512 devices in a mesh: seq: 8 (over x, core), exp: 64 (over z, y).
Axes of the slice: x: 4, y: 8, z: 8, core: 2. Of those that a mesh axis runs over, the one named last changes fastest.
Arguments:
- tokens: bfloat16 [64, 2048, 1280], P('exp', 'seq'), may hold values from -14 to 14
- slot_keys: bfloat16 [1280, 256], P('seq'), may hold values from -1 to 1
- expert_in: bfloat16 [64, 1280, 5120], P('exp', None, 'seq'), may hold values from -0.3125 to 0.3125
- expert_out: bfloat16 [64, 5120, 1280], P('exp', 'seq'), may hold values from -0.15625 to 0.15625
Outputs:
- mixed: bfloat16 [64, 2048, 1280], P('exp', 'seq')
The draws below stay inside these ranges and needn't reach their ends.
All inputs are finite; a program needn't handle non-finite values.
Results may differ from the reference program's by a relative error of at most 0.029.
Values may be sent and summed in bfloat16 or wider, within the bound.
A program may use at most 64 MiB of HBM per device.

```python
import math
import jax
import jax.numpy as jnp
from jax import lax

D = 1280
EXPERTS = 256
FF = 5120
PATCH_DEV = 256
IMAGES = 64
PATCHES = 2048
WINDOW = 64
N_SEQ = 8


def slot_table(key):
    return jax.random.truncated_normal(key, -2.0, 2.0, (D, EXPERTS), jnp.float32) * (2.5 / math.sqrt(D))


def draw_slot_keys(key, part):
    return slot_table(key).astype(jnp.bfloat16)


def draw_tokens(key, part):
    key = jax.random.fold_in(key, 7)
    return jax.random.truncated_normal(key, -6.0, 6.0, (IMAGES, PATCHES, D), jnp.float32).astype(jnp.bfloat16)


def block_scale(key, dims, pieces, low, largest):
    gain, own = 1.0, jax.random.fold_in(key, 6)
    for position, parts in pieces:
        heights = jnp.exp(jax.random.uniform(jax.random.fold_in(own, position), (parts,), jnp.float32, low / len(pieces), largest / len(pieces)))
        gain = gain * jnp.repeat(heights, dims[position] // parts).reshape([-1 if axis == position else 1 for axis in range(len(dims))])
    return gain


def normal_values(rng, shape, deviation, most, shards=(), held_as=jnp.bfloat16):
    values = jax.random.normal(rng, shape, jnp.float32) * deviation
    if len(shards) > 0:
        values = block_scale(rng, shape, shards, -0.22, 0.18) * values
    return jnp.clip(values, min=-most, max=most).astype(held_as)


def setup_inputs(seed: int = 0) -> dict:
    splits = jax.random.split(jax.random.key(seed), 5)
    return {
        "tokens": draw_tokens(jax.random.fold_in(splits[4], 71), 0),
        "slot_keys": draw_slot_keys(jax.random.fold_in(splits[4], 71), 0),
        "expert_in": normal_values(splits[2], (WINDOW, D, FF), (D // 4) ** -0.5, 0.3125, ((0, 64), (2, 8))),
        "expert_out": normal_values(splits[3], (WINDOW, FF, D), (FF // 4) ** -0.5, 0.15625, ((0, 64), (1, 8))),
    }


def bf16_round(values):
    return lax.optimization_barrier(values.astype(jnp.bfloat16)).astype(jnp.float32)


def reference(tokens, slot_keys, expert_in, expert_out):
    def image_work(image_tokens):
        scores = jnp.dot(image_tokens, slot_keys, preferred_element_type=jnp.float32)
        combine = jax.nn.softmax(scores, axis=1)[:, :WINDOW].astype(jnp.bfloat16)
        dispatch = jax.nn.softmax(scores[:, :WINDOW], axis=0).astype(jnp.bfloat16)
        block_weights = dispatch.reshape(N_SEQ, PATCH_DEV, WINDOW).astype(jnp.float32)
        block_tokens = image_tokens.reshape(N_SEQ, PATCH_DEV, D).astype(jnp.float32)
        partial_value = jnp.einsum("spk,spd->skd", block_weights, block_tokens)
        slot_inputs = jnp.sum(bf16_round(partial_value), axis=0).astype(jnp.bfloat16)
        return slot_inputs, combine

    slot_inputs, combine = lax.map(image_work, tokens)
    hidden_block = FF // N_SEQ

    def expert_work(operands):
        inputs, first_w, second_w = operands
        pre_act = jnp.dot(inputs, first_w, preferred_element_type=jnp.float32)
        hidden = jax.nn.gelu(pre_act, approximate=True).astype(jnp.bfloat16)
        hidden_blocks = hidden.reshape(IMAGES, N_SEQ, hidden_block).astype(jnp.float32)
        weight_blocks = second_w.reshape(N_SEQ, hidden_block, D).astype(jnp.float32)
        partial_value = jnp.einsum("isf,sfd->sid", hidden_blocks, weight_blocks)
        return jnp.sum(bf16_round(partial_value), axis=0).astype(jnp.bfloat16)

    slot_outputs = lax.map(expert_work, (jnp.swapaxes(slot_inputs, 0, 1), expert_in, expert_out))

    def mix_work(operands):
        weights, outputs = operands
        return jnp.dot(weights, outputs, preferred_element_type=jnp.float32).astype(jnp.bfloat16)

    return lax.map(mix_work, (combine, jnp.swapaxes(slot_outputs, 0, 1)))
```

```python
import jax
import jax.numpy as jnp
from jax import lax
from jax.experimental import pallas as pl
from jax.experimental.pallas import tpu as pltpu
from jax.sharding import PartitionSpec as P

MESH = pl.DeviceIdType.MESH
BF = jnp.bfloat16
F32 = jnp.float32
SEQ = 8
SIDE = 8
D = 1280
HID = 640
PATCH = 256
SLOTS = 256
WINDOW = 64
ROWS = D // SEQ
HALF = D // 2
PACK = ROWS // 2
REST = PACK + ROWS
LINE = 16
TILES = D // 128
NEAR = (4, 5, 3, 6, 2, 7, 1)


def wait_bytes(ref, sem):
    pltpu.make_async_copy(ref, ref, sem).wait()


def gelu(v):
    inner = 0.7978845608028654 * (v + 0.044715 * (v * v * v))
    return 0.5 * v * (1.0 + jnp.tanh(inner))


def kernel(
    tok_hbm, keys_hbm, w1_hbm, w2_hbm, out_hbm,
    tok, keys, w1, w2, outv,
    ka_send, ka_recv, kb_send, kb_recv, kfull,
    st_send, st_recv, p_send, p_recv, q_send, q_recv,
    stage, r_send, r2_send, x_recv, y_recv, wide, xv, comb,
    load_sem, out_sem, ysem, zsem,
    ka_s, ka_r, kb_s, kb_r, kf_s, kf_r, st_s, st_r, p_s, p_r, q_s, q_r, x_s, x_r, y_s, y_r,
):
    s = lax.axis_index("seq")
    e = lax.axis_index("exp")
    z = e // SIDE
    y = lax.rem(e, SIDE)
    mine = lax.rem(s - z + SIDE, SIDE)

    def seq_peers():
        return [lax.rem(s + d, SEQ) for d in NEAR]

    def group_of(peer):
        return lax.rem(peer - z + SIDE, SIDE)

    loads = [
        pltpu.make_async_copy(keys_hbm, keys, load_sem.at[0]),
        pltpu.make_async_copy(tok_hbm.at[0], tok, load_sem.at[1]),
        pltpu.make_async_copy(w1_hbm.at[0], w1, load_sem.at[2]),
        pltpu.make_async_copy(w2_hbm.at[0], w2, load_sem.at[3]),
    ]
    barrier = pltpu.get_barrier_semaphore()
    for d in NEAR:
        pl.semaphore_signal(barrier, inc=1, device_id=(s, z * SIDE + lax.rem(y + d, SIDE)), device_id_type=MESH)
        pl.semaphore_signal(barrier, inc=1, device_id=(s, lax.rem(z + d, SIDE) * SIDE + y), device_id_type=MESH)
        pl.semaphore_signal(barrier, inc=1, device_id=(lax.rem(s + d, SEQ), e), device_id_type=MESH)
    for load in loads:
        load.start()
    stage[...] = jnp.zeros_like(stage)

    loads[0].wait()
    kk = keys[...]
    ka = jnp.concatenate([kk[:PACK, :WINDOW], kk[PACK:, :WINDOW]], axis=1)
    ka_send[...] = ka
    ka_recv[s] = ka
    kb_send[:PACK] = jnp.concatenate([kk[:PACK, WINDOW:128], kk[PACK:, WINDOW:128]], axis=1)
    kb_send[PACK:] = kk[:, 128:]
    kb_recv[s] = kb_send[...]
    pl.semaphore_wait(barrier, 21)

    def remote(src, dst, ssem, rsem, seq, exp):
        return pltpu.make_async_remote_copy(
            src_ref=src, dst_ref=dst, send_sem=ssem, recv_sem=rsem, device_id=(seq, exp), device_id_type=MESH
        )

    for peer in seq_peers():
        remote(ka_send, ka_recv.at[s], ka_s, ka_r, peer, e).start()
    for peer in seq_peers():
        remote(kb_send, kb_recv.at[s], kb_s, kb_r, peer, e).start()
    for d in NEAR:
        pl.semaphore_signal(ysem, inc=1, device_id=(s, z * SIDE + lax.rem(y + d, SIDE)), device_id_type=MESH)
    loads[1].wait()
    wait_bytes(ka_recv.at[pl.ds(0, SEQ - 1)], ka_r)
    for src in range(SEQ):
        got = ka_recv[src]
        kfull[ROWS * src : ROWS * src + PACK, :WINDOW] = got[:, :WINDOW]
        kfull[ROWS * src + PACK : ROWS * (src + 1), :WINDOW] = got[:, WINDOW:]

    scores = jnp.dot(tok[...], kfull[:, :WINDOW], preferred_element_type=F32)
    scores_t = scores.T
    top = jnp.max(scores_t, axis=1, keepdims=True)
    raised = jnp.exp(scores_t - top)
    total = jnp.sum(raised, axis=1, keepdims=True)
    lane = lax.broadcasted_iota(jnp.int32, (WINDOW, 128), 1)
    st_send[...] = jnp.where(lane < 64, top, total)
    for peer in seq_peers():
        rows = pl.ds(pl.multiple_of(group_of(peer) * SIDE, SIDE), SIDE)
        remote(st_send.at[rows], st_recv.at[s], st_s, st_r, peer, e).start()
    st_recv[s] = st_send[pl.ds(pl.multiple_of(mine * SIDE, SIDE), SIDE)]
    part = jnp.dot(raised.astype(BF), tok[...], preferred_element_type=F32)
    part = part * (1.0 / total)

    def fold(values, ref):
        for g in range(SIDE):
            block = values[g * SIDE : (g + 1) * SIDE]
            ref[g] = jnp.concatenate([block[:, :HALF], block[:, HALF:]], axis=0).astype(BF)

    def to_owners(send, recv, ssem, rsem):
        for peer in seq_peers():
            remote(send.at[group_of(peer)], recv.at[s], ssem, rsem, peer, e).start()
        recv[s] = send[mine]

    def to_lines(low, high, ref):
        for t in range(TILES):
            half = low if t < TILES // 2 else high
            c = (t % (TILES // 2)) * 128
            stage[pl.ds(t, SIDE, stride=LINE), :] = half[:, c : c + 128]
        ref[...] = stage[: SIDE * LINE].astype(BF)

    def spread(send, recv, ssem, rsem):
        x = s // 2
        here = pl.ds(pl.multiple_of(e * LINE, LINE), LINE)

        def step(j, carry):
            off = 4 + ((j + 1) // 2) * (2 * lax.rem(j, 2) - 1)
            row = lax.rem(y + off + SIDE, SIDE)
            src = send.at[pl.ds(pl.multiple_of(row * LINE, LINE), LINE)]
            to = mine * SIDE + row
            for dx in (2, 1, 3, 0):
                for core in range(2):
                    seq = lax.rem(x + dx, 4) * 2 + core
                    if dx:
                        remote(src, recv.at[here], ssem, rsem, seq, to).start()
                    else:
                        itself = jnp.logical_and(seq == s, to == e)

                        @pl.when(jnp.logical_not(itself))
                        def _():
                            remote(src, recv.at[here], ssem, rsem, seq, to).start()

                        @pl.when(itself)
                        def _():
                            pltpu.make_async_copy(src, recv.at[here], rsem).start()

            return carry

        lax.fori_loop(0, SIDE, step, 0)

    def spread_sent(recv, ssem):
        @pl.when(mine == z)
        def _():
            wait_bytes(recv.at[pl.ds(0, 63 * LINE)], ssem)

        @pl.when(mine != z)
        def _():
            wait_bytes(recv, ssem)

    def gather_lines(recv):
        wide[: 64 * LINE] = recv[...].astype(F32)
        for t in range(TILES):
            xv[:, 128 * t : 128 * (t + 1)] = wide[pl.ds(t, 64, stride=LINE), :].astype(BF)

    fold(part, p_send)
    to_owners(p_send, p_recv, p_s, p_r)
    pl.semaphore_wait(ysem, 7)
    for d in NEAR:
        pl.semaphore_signal(zsem, inc=1, device_id=(s, lax.rem(z + d, SIDE) * SIDE + y), device_id_type=MESH)

    wait_bytes(st_recv.at[pl.ds(0, SEQ - 1)], st_r)
    tops = [st_recv[i][:, 0:1] for i in range(SEQ)]
    sums = [st_recv[i][:, 64:65] for i in range(SEQ)]
    peak = tops[0]
    for i in range(1, SEQ):
        peak = jnp.maximum(peak, tops[i])
    weights = [jnp.exp(tops[i] - peak) * sums[i] for i in range(SEQ)]
    norm = weights[0]
    for i in range(1, SEQ):
        norm = norm + weights[i]
    norm = 1.0 / norm
    wait_bytes(p_recv.at[pl.ds(0, SEQ - 1)], p_r)
    low = high = None
    for i in range(SEQ):
        got = p_recv[i].astype(F32)
        w = weights[i] * norm
        a, b = got[:SIDE] * w, got[SIDE:] * w
        low, high = (a, b) if low is None else (low + a, high + b)
    to_lines(low, high, r_send)
    pl.semaphore_wait(zsem, 7)
    spread(r_send, x_recv, x_s, x_r)

    wait_bytes(kb_recv.at[pl.ds(0, SEQ - 1)], kb_r)
    for src in range(SEQ):
        got = kb_recv[src]
        kfull[ROWS * src : ROWS * src + PACK, WINDOW:128] = got[:PACK, :WINDOW]
        kfull[ROWS * src + PACK : ROWS * (src + 1), WINDOW:128] = got[:PACK, WINDOW:]
        kfull[ROWS * src : ROWS * (src + 1), 128:] = got[PACK:]
    every = jnp.dot(tok[...], kfull[...], preferred_element_type=F32)
    up = jnp.exp(every - jnp.max(every, axis=1, keepdims=True))
    comb[...] = (up[:, :WINDOW] * (1.0 / jnp.sum(up, axis=1, keepdims=True))).astype(BF)

    loads[2].wait()
    loads[3].wait()
    wait_bytes(x_recv, x_r)
    gather_lines(x_recv)
    hidden = gelu(jnp.dot(xv[...], w1[...], preferred_element_type=F32)).astype(BF)
    fold(jnp.dot(hidden, w2[...], preferred_element_type=F32), q_send)
    to_owners(q_send, q_recv, q_s, q_r)
    wait_bytes(q_recv.at[pl.ds(0, SEQ - 1)], q_r)
    low = high = None
    for i in range(SEQ):
        got = q_recv[i].astype(F32)
        a, b = got[:SIDE], got[SIDE:]
        low, high = (a, b) if low is None else (low + a, high + b)
    to_lines(low, high, r2_send)
    spread(r2_send, y_recv, y_s, y_r)
    wait_bytes(ka_recv.at[pl.ds(0, SEQ - 1)], ka_s)
    wait_bytes(kb_recv.at[pl.ds(0, SEQ - 1)], kb_s)
    wait_bytes(st_recv.at[pl.ds(0, SEQ - 1)], st_s)
    wait_bytes(p_recv.at[pl.ds(0, SEQ - 1)], p_s)
    wait_bytes(q_recv.at[pl.ds(0, SEQ - 1)], q_s)
    spread_sent(x_recv, x_s)

    wait_bytes(y_recv, y_r)
    gather_lines(y_recv)
    outs = []
    for c in range(5):
        cols = slice(256 * c, 256 * (c + 1))
        outv[:, cols] = jnp.dot(comb[...], xv[:, cols], preferred_element_type=F32).astype(BF)
        copy = pltpu.make_async_copy(outv.at[:, cols], out_hbm.at[0, :, cols], out_sem.at[c])
        copy.start()
        outs.append(copy)
    spread_sent(y_recv, y_s)
    for copy in outs:
        copy.wait()


def on_device(tokens, slot_keys, expert_in, expert_out):
    dma = pltpu.SemaphoreType.DMA
    reg = pltpu.SemaphoreType.REGULAR
    vm = pltpu.VMEM
    scratch = [
        vm((PATCH, D), BF), vm((ROWS, SLOTS), BF), vm((D, HID), BF), vm((HID, D), BF), vm((PATCH, D), BF),
        vm((PACK, 128), BF), vm((SEQ, PACK, 128), BF), vm((REST, 128), BF), vm((SEQ, REST, 128), BF), vm((D, SLOTS), BF),
        vm((WINDOW, 128), F32), vm((SEQ, SIDE, 128), F32),
        vm((SIDE, 16, HALF), BF), vm((SEQ, 16, HALF), BF), vm((SIDE, 16, HALF), BF), vm((SEQ, 16, HALF), BF),
        vm(((SIDE + 1) * LINE, 128), F32), vm((SIDE * LINE, 128), BF), vm((SIDE * LINE, 128), BF),
        vm((64 * LINE, 128), BF), vm((64 * LINE, 128), BF), vm((65 * LINE, 128), F32), vm((64, D), BF), vm((PATCH, WINDOW), BF),
        dma((4,)), dma((5,)), reg, reg,
    ] + [dma] * 16
    anywhere = pl.BlockSpec(memory_space=pl.ANY)
    return pl.pallas_call(
        kernel,
        name="moe",
        out_shape=jax.ShapeDtypeStruct(tokens.shape, BF),
        in_specs=[anywhere] * 4,
        out_specs=anywhere,
        scratch_shapes=scratch,
        compiler_params=pltpu.CompilerParams(collective_id=0, has_side_effects=True, vmem_limit_bytes=48 * 1024 * 1024),
    )(tokens, slot_keys, expert_in, expert_out)


def solution(mesh):
    return jax.shard_map(
        on_device,
        mesh=mesh,
        in_specs=(
            P("exp", "seq", None),
            P("seq", None),
            P("exp", None, "seq"),
            P("exp", "seq", None),
        ),
        out_specs=P("exp", "seq", None),
        check_vma=False,
    )
```

```python
import jax
import jax.numpy as jnp
from jax import lax
from jax.experimental import pallas as pl
from jax.experimental.pallas import tpu as pltpu
from jax.sharding import PartitionSpec as P

MESH = pl.DeviceIdType.MESH
BF = jnp.bfloat16
F32 = jnp.float32
SEQ = 8
SIDE = 8
D = 1280
HID = 640
PATCH = 256
SLOTS = 256
WINDOW = 64
ROWS = D // SEQ
HALF = D // 2
PACK = ROWS // 2
REST = PACK + ROWS
LINE = 16
TILES = D // 128
NEAR = (4, 5, 3, 6, 2, 7, 1)


def wait_bytes(ref, sem):
    pltpu.make_async_copy(ref, ref, sem).wait()


def gelu(v):
    inner = 0.7978845608028654 * (v + 0.044715 * (v * v * v))
    return 0.5 * v * (1.0 + jnp.tanh(inner))


def kernel(
    tok_hbm, keys_hbm, w1_hbm, w2_hbm, out,
    tok, keys, w1, w2,
    ka_send, ka_recv, kb_send, kb_recv, kfull,
    st_send, st_recv, p_send, p_recv, q_send, q_recv,
    stage, r1_send, r2_send, b1_recv, b2_recv, c1_recv, c2_recv, xv, comb,
    load_sem, ysem, zsem, wsem,
    ka_s, ka_r, kb_s, kb_r, kf_s, kf_r, st_s, st_r, p_s, p_r, q_s, q_r,
    b1_s, b1_r, b2_s, b2_r, c1_s, c1_r, c2_s, c2_r,
):
    s = lax.axis_index("seq")
    e = lax.axis_index("exp")
    x, core = s // 2, lax.rem(s, 2)
    z, y = e // SIDE, lax.rem(e, SIDE)
    mine = lax.rem(s - z + SIDE, SIDE)

    def along_y(d):
        return (s, z * SIDE + lax.rem(y + d, SIDE))

    def along_z(d):
        return (s, lax.rem(z + d, SIDE) * SIDE + y)

    def along_seq(d):
        return (lax.rem(s + d, SEQ), e)

    def signal(sem, device):
        pl.semaphore_signal(sem, inc=1, device_id=device, device_id_type=MESH)

    def remote(src, dst, ssem, rsem, device):
        return pltpu.make_async_remote_copy(
            src_ref=src, dst_ref=dst, send_sem=ssem, recv_sem=rsem, device_id=device, device_id_type=MESH
        )

    def group_of(d):
        return lax.rem(s + d - z + SIDE, SIDE)

    barrier = pltpu.get_barrier_semaphore()
    for d in NEAR:
        signal(barrier, along_seq(d))
    for d in (2, 6, 1, 7):
        signal(barrier, along_y(d))
        signal(barrier, along_z(d))
    loads = [
        pltpu.make_async_copy(keys_hbm, keys, load_sem.at[0]),
        pltpu.make_async_copy(tok_hbm.at[0], tok, load_sem.at[1]),
        pltpu.make_async_copy(w1_hbm.at[0], w1, load_sem.at[2]),
        pltpu.make_async_copy(w2_hbm.at[0], w2, load_sem.at[3]),
    ]
    for load in loads:
        load.start()
    stage[...] = jnp.zeros_like(stage)

    loads[0].wait()
    kk = keys[...]
    ka = jnp.concatenate([kk[:PACK, :WINDOW], kk[PACK:, :WINDOW]], axis=1)
    ka_send[...] = ka
    ka_recv[s] = ka
    kb_send[:PACK] = jnp.concatenate([kk[:PACK, WINDOW:128], kk[PACK:, WINDOW:128]], axis=1)
    kb_send[PACK:] = kk[:, 128:]
    kb_recv[core, x] = kb_send[...]
    pl.semaphore_wait(barrier, 15)
    for d in NEAR:
        remote(ka_send, ka_recv.at[s], ka_s, ka_r, along_seq(d)).start()
    for d in (2, 6):
        signal(ysem, along_y(d))
        signal(zsem, along_z(d))
    loads[1].wait()
    wait_bytes(ka_recv.at[pl.ds(0, SEQ - 1)], ka_r)
    for src in range(SEQ):
        got = ka_recv[src]
        kfull[ROWS * src : ROWS * src + PACK, :WINDOW] = got[:, :WINDOW]
        kfull[ROWS * src + PACK : ROWS * (src + 1), :WINDOW] = got[:, WINDOW:]

    scores = jnp.dot(tok[...], kfull[:, :WINDOW], preferred_element_type=F32)
    scores_t = scores.T
    top = jnp.max(scores_t, axis=1, keepdims=True)
    raised = jnp.exp(scores_t - top)
    total = jnp.sum(raised, axis=1, keepdims=True)
    lane = lax.broadcasted_iota(jnp.int32, (WINDOW, 128), 1)
    st_send[...] = jnp.where(lane < 64, top, total)
    for d in NEAR:
        rows = pl.ds(pl.multiple_of(group_of(d) * SIDE, SIDE), SIDE)
        remote(st_send.at[rows], st_recv.at[s], st_s, st_r, along_seq(d)).start()
    st_recv[s] = st_send[pl.ds(pl.multiple_of(mine * SIDE, SIDE), SIDE)]
    part = jnp.dot(raised.astype(BF), tok[...], preferred_element_type=F32)
    part = part * (1.0 / total)

    def fold(values, ref):
        for g in range(SIDE):
            block = values[g * SIDE : (g + 1) * SIDE]
            ref[g] = jnp.concatenate([block[:, :HALF], block[:, HALF:]], axis=0).astype(BF)

    def to_owners(send, recv, ssem, rsem):
        for d in NEAR:
            remote(send.at[group_of(d)], recv.at[s], ssem, rsem, along_seq(d)).start()
        recv[s] = send[mine]

    def exchange(low, high, send, recv, ssem, rsem):
        for t in range(TILES):
            half = low if t < TILES // 2 else high
            c = (t % (TILES // 2)) * 128
            stage[pl.ds(t, SIDE, stride=LINE), :] = half[:, c : c + 128]
        send[...] = stage[: SIDE * LINE].astype(BF)
        here = recv.at[pl.ds(pl.multiple_of(y * LINE, LINE), LINE)]
        for d in NEAR:
            row = lax.rem(y + d, SIDE)
            src = send.at[pl.ds(pl.multiple_of(row * LINE, LINE), LINE)]
            remote(src, here, ssem, rsem, (s, mine * SIDE + row)).start()
        src = send.at[pl.ds(pl.multiple_of(y * LINE, LINE), LINE)]

        @pl.when(mine != z)
        def _():
            remote(src, here, ssem, rsem, (s, mine * SIDE + y)).start()

        @pl.when(mine == z)
        def _():
            pltpu.make_async_copy(src, here, rsem).start()

    def exchanged(recv, ssem):
        @pl.when(mine != z)
        def _():
            wait_bytes(recv, ssem)

        @pl.when(mine == z)
        def _():
            wait_bytes(recv.at[pl.ds(0, 7 * LINE)], ssem)

    def share(lines, recv, ssem, rsem):
        stage[: SIDE * LINE] = lines[...].astype(F32)
        parts = [stage[pl.ds(t, SIDE, stride=LINE), :] for t in range(TILES)]
        low = jnp.concatenate(parts[: TILES // 2], axis=1)
        high = jnp.concatenate(parts[TILES // 2 :], axis=1)
        recv[s] = jnp.concatenate([low, high], axis=0).astype(BF)
        for d in NEAR:
            remote(recv.at[s], recv.at[s], ssem, rsem, along_seq(d)).start()

    def unfold(recv):
        for g in range(0, SIDE, 2):
            a = recv[lax.rem(g + z, SIDE)].astype(F32)
            b = recv[lax.rem(g + 1 + z, SIDE)].astype(F32)
            rows = slice(g * SIDE, (g + 2) * SIDE)
            xv[rows, :HALF] = jnp.concatenate([a[:SIDE], b[:SIDE]], axis=0).astype(BF)
            xv[rows, HALF:] = jnp.concatenate([a[SIDE:], b[SIDE:]], axis=0).astype(BF)

    fold(part, p_send)
    to_owners(p_send, p_recv, p_s, p_r)
    pl.semaphore_wait(ysem, 2)
    pl.semaphore_wait(zsem, 2)

    @pl.when(mine != z)
    def _():
        signal(wsem, (s, mine * SIDE + y))

    wait_bytes(st_recv.at[pl.ds(0, SEQ - 1)], st_r)
    tops = [st_recv[i][:, 0:1] for i in range(SEQ)]
    sums = [st_recv[i][:, 64:65] for i in range(SEQ)]
    peak = tops[0]
    for i in range(1, SEQ):
        peak = jnp.maximum(peak, tops[i])
    weights = [jnp.exp(tops[i] - peak) * sums[i] for i in range(SEQ)]
    norm = weights[0]
    for i in range(1, SEQ):
        norm = norm + weights[i]
    norm = 1.0 / norm

    @pl.when(mine != z)
    def _():
        pl.semaphore_wait(wsem, 1)

    wait_bytes(p_recv.at[pl.ds(0, SEQ - 1)], p_r)
    low = high = None
    for i in range(SEQ):
        got = p_recv[i].astype(F32)
        w = weights[i] * norm
        a, b = got[:SIDE] * w, got[SIDE:] * w
        low, high = (a, b) if low is None else (low + a, high + b)
    exchange(low, high, r1_send, b1_recv, b1_s, b1_r)
    for d in (4, 2, 6):
        remote(kb_send, kb_recv.at[core, x], kb_s, kb_r, along_seq(d)).start()
    wait_bytes(b1_recv, b1_r)
    share(b1_recv, c1_recv, c1_s, c1_r)
    loads[2].wait()
    loads[3].wait()
    wait_bytes(c1_recv.at[pl.ds(0, SEQ - 1)], c1_r)

    unfold(c1_recv)
    hidden = gelu(jnp.dot(xv[...], w1[...], preferred_element_type=F32)).astype(BF)
    fold(jnp.dot(hidden, w2[...], preferred_element_type=F32), q_send)
    to_owners(q_send, q_recv, q_s, q_r)
    wait_bytes(q_recv.at[pl.ds(0, SEQ - 1)], q_r)
    low = high = None
    for i in range(SEQ):
        got = q_recv[i].astype(F32)
        a, b = got[:SIDE], got[SIDE:]
        low, high = (a, b) if low is None else (low + a, high + b)
    exchange(low, high, r2_send, b2_recv, b2_s, b2_r)

    wait_bytes(kb_recv.at[0, pl.ds(0, 3)], kb_r)
    forward = remote(kb_recv.at[core], kb_recv.at[core], kf_s, kf_r, (s + 1 - 2 * core, e))
    forward.start()
    forward.wait()
    for src in range(SEQ):
        got = kb_recv[src % 2, src // 2]
        kfull[ROWS * src : ROWS * src + PACK, WINDOW:128] = got[:PACK, :WINDOW]
        kfull[ROWS * src + PACK : ROWS * (src + 1), WINDOW:128] = got[:PACK, WINDOW:]
        kfull[ROWS * src : ROWS * (src + 1), 128:] = got[PACK:]
    every = jnp.dot(tok[...], kfull[...], preferred_element_type=F32)
    up = jnp.exp(every - jnp.max(every, axis=1, keepdims=True))
    comb[...] = (up[:, :WINDOW] * (1.0 / jnp.sum(up, axis=1, keepdims=True))).astype(BF)

    wait_bytes(b2_recv, b2_r)
    share(b2_recv, c2_recv, c2_s, c2_r)
    wait_bytes(ka_recv.at[pl.ds(0, SEQ - 1)], ka_s)
    wait_bytes(kb_recv.at[0, pl.ds(0, 3)], kb_s)
    wait_bytes(st_recv.at[pl.ds(0, SEQ - 1)], st_s)
    wait_bytes(p_recv.at[pl.ds(0, SEQ - 1)], p_s)
    wait_bytes(q_recv.at[pl.ds(0, SEQ - 1)], q_s)
    exchanged(b1_recv, b1_s)
    exchanged(b2_recv, b2_s)
    wait_bytes(c1_recv.at[pl.ds(0, SEQ - 1)], c1_s)

    wait_bytes(c2_recv.at[pl.ds(0, SEQ - 1)], c2_r)
    unfold(c2_recv)
    for c in range(5):
        cols = slice(256 * c, 256 * (c + 1))
        out[0, :, cols] = jnp.dot(comb[...], xv[:, cols], preferred_element_type=F32).astype(BF)
    wait_bytes(c2_recv.at[pl.ds(0, SEQ - 1)], c2_s)


def on_device(tokens, slot_keys, expert_in, expert_out):
    dma = pltpu.SemaphoreType.DMA
    reg = pltpu.SemaphoreType.REGULAR
    vm = pltpu.VMEM
    lines, folded = (SIDE * LINE, 128), (SEQ, 16, HALF)
    scratch = [
        vm((PATCH, D), BF), vm((ROWS, SLOTS), BF), vm((D, HID), BF), vm((HID, D), BF),
        vm((PACK, 128), BF), vm((SEQ, PACK, 128), BF), vm((REST, 128), BF), vm((2, 4, REST, 128), BF), vm((D, SLOTS), BF),
        vm((WINDOW, 128), F32), vm((SEQ, SIDE, 128), F32), vm(folded, BF), vm(folded, BF), vm(folded, BF), vm(folded, BF),
        vm(((SIDE + 1) * LINE, 128), F32), vm(lines, BF), vm(lines, BF), vm(lines, BF), vm(lines, BF),
        vm(folded, BF), vm(folded, BF), vm((64, D), BF), vm((PATCH, WINDOW), BF),
        dma((4,)), reg, reg, reg,
    ] + [dma] * 20
    operands = [pltpu.with_memory_space_constraint(a, pltpu.HBM) for a in (tokens, slot_keys, expert_in, expert_out)]
    return pl.pallas_call(
        kernel,
        name="moe",
        out_shape=jax.ShapeDtypeStruct(tokens.shape, BF),
        in_specs=[pl.BlockSpec(memory_space=pl.ANY)] * 4,
        out_specs=pl.BlockSpec(memory_space=pltpu.VMEM),
        scratch_shapes=scratch,
        compiler_params=pltpu.CompilerParams(collective_id=0, has_side_effects=True, vmem_limit_bytes=48 * 1024 * 1024),
    )(*operands)


def solution(mesh):
    return jax.shard_map(
        on_device,
        mesh=mesh,
        in_specs=(
            P("exp", "seq", None),
            P("seq", None),
            P("exp", None, "seq"),
            P("exp", "seq", None),
        ),
        out_specs=P("exp", "seq", None),
        check_vma=False,
    )
```

```python
import jax
import jax.numpy as jnp
from jax import lax
from jax.experimental import pallas as pl
from jax.experimental.pallas import tpu as pltpu
from jax.sharding import PartitionSpec as P

MESH = pl.DeviceIdType.MESH
BF = jnp.bfloat16
F32 = jnp.float32
SEQ = 8
SIDE = 8
D = 1280
HID = 640
PATCH = 256
SLOTS = 256
WINDOW = 64
ROWS = D // SEQ
HALF = D // 2
PACK = ROWS // 2
REST = PACK + ROWS
LINE = 16
TILES = D // 128
NEAR = (4, 5, 3, 6, 2, 7, 1)


def wait_bytes(ref, sem):
    pltpu.make_async_copy(ref, ref, sem).wait()


def gelu(v):
    inner = 0.7978845608028654 * (v + 0.044715 * (v * v * v))
    return 0.5 * v * (1.0 + jnp.tanh(inner))


def kernel(
    tok_hbm, keys_hbm, w1_hbm, w2_hbm, comb, mixed_in,
    tok, keys, w1, w2,
    ka_send, ka_recv, kb_send, kb_recv, kfull,
    st_send, st_recv, p_send, p_recv, q_send, q_recv,
    stage, wide, r1_send, r2_send, c1_recv, c2_recv, xv,
    load_sem, ysem, zsem, wsem,
    ka_s, ka_r, kb_s, kb_r, kf_s, kf_r, st_s, st_r, p_s, p_r, q_s, q_r,
    b1_s, b1_r, b2_s, b2_r, c1_s, c1_r, c2_s, c2_r,
):
    s = lax.axis_index("seq")
    e = lax.axis_index("exp")
    x, core = s // 2, lax.rem(s, 2)
    z, y = e // SIDE, lax.rem(e, SIDE)
    mine = lax.rem(s - z + SIDE, SIDE)

    def along_y(d):
        return (s, z * SIDE + lax.rem(y + d, SIDE))

    def along_z(d):
        return (s, lax.rem(z + d, SIDE) * SIDE + y)

    def along_seq(d):
        return (lax.rem(s + d, SEQ), e)

    def signal(sem, device):
        pl.semaphore_signal(sem, inc=1, device_id=device, device_id_type=MESH)

    def remote(src, dst, ssem, rsem, device):
        return pltpu.make_async_remote_copy(
            src_ref=src, dst_ref=dst, send_sem=ssem, recv_sem=rsem, device_id=device, device_id_type=MESH
        )

    def group_of(d):
        return lax.rem(s + d - z + SIDE, SIDE)

    barrier = pltpu.get_barrier_semaphore()
    for d in NEAR:
        signal(barrier, along_seq(d))
    for d in (2, 6, 1, 7):
        signal(barrier, along_y(d))
        signal(barrier, along_z(d))
    loads = [
        pltpu.make_async_copy(keys_hbm, keys, load_sem.at[0]),
        pltpu.make_async_copy(tok_hbm.at[0], tok, load_sem.at[1]),
        pltpu.make_async_copy(w1_hbm.at[0], w1, load_sem.at[2]),
        pltpu.make_async_copy(w2_hbm.at[0], w2, load_sem.at[3]),
    ]
    for load in loads:
        load.start()
    stage[...] = jnp.zeros_like(stage)

    loads[0].wait()
    kk = keys[...]
    ka = jnp.concatenate([kk[:PACK, :WINDOW], kk[PACK:, :WINDOW]], axis=1)
    ka_send[...] = ka
    ka_recv[s] = ka
    kb_send[:PACK] = jnp.concatenate([kk[:PACK, WINDOW:128], kk[PACK:, WINDOW:128]], axis=1)
    kb_send[PACK:] = kk[:, 128:]
    kb_recv[core, x] = kb_send[...]
    pl.semaphore_wait(barrier, 15)
    for d in NEAR:
        remote(ka_send, ka_recv.at[s], ka_s, ka_r, along_seq(d)).start()
    for d in (2, 6):
        signal(ysem, along_y(d))
        signal(zsem, along_z(d))
    loads[1].wait()
    wait_bytes(ka_recv.at[pl.ds(0, SEQ - 1)], ka_r)
    for src in range(SEQ):
        got = ka_recv[src]
        kfull[ROWS * src : ROWS * src + PACK, :WINDOW] = got[:, :WINDOW]
        kfull[ROWS * src + PACK : ROWS * (src + 1), :WINDOW] = got[:, WINDOW:]

    scores = jnp.dot(tok[...], kfull[:, :WINDOW], preferred_element_type=F32)
    scores_t = scores.T
    top = jnp.max(scores_t, axis=1, keepdims=True)
    raised = jnp.exp(scores_t - top)
    total = jnp.sum(raised, axis=1, keepdims=True)
    lane = lax.broadcasted_iota(jnp.int32, (WINDOW, 128), 1)
    st_send[...] = jnp.where(lane < 64, top, total)
    for d in NEAR:
        rows = pl.ds(pl.multiple_of(group_of(d) * SIDE, SIDE), SIDE)
        remote(st_send.at[rows], st_recv.at[s], st_s, st_r, along_seq(d)).start()
    st_recv[s] = st_send[pl.ds(pl.multiple_of(mine * SIDE, SIDE), SIDE)]
    part = jnp.dot(raised.astype(BF), tok[...], preferred_element_type=F32)
    part = part * (1.0 / total)

    def fold(values, ref):
        for g in range(SIDE):
            block = values[g * SIDE : (g + 1) * SIDE]
            ref[g] = jnp.concatenate([block[:, :HALF], block[:, HALF:]], axis=0).astype(BF)

    def to_owners(send, recv, ssem, rsem):
        for d in NEAR:
            remote(send.at[group_of(d)], recv.at[s], ssem, rsem, along_seq(d)).start()
        recv[s] = send[mine]

    def line(row):
        return pl.ds(pl.multiple_of(row * LINE, LINE), LINE)

    def exchange(low, high, send, recv, ssem, rsem):
        for t in range(TILES):
            half = low if t < TILES // 2 else high
            c = (t % (TILES // 2)) * 128
            stage[pl.ds(t, SIDE, stride=LINE), :] = half[:, c : c + 128]
        send[...] = stage[: SIDE * LINE].astype(BF)
        here = recv.at[line(e)]
        for d in NEAR:
            row = lax.rem(y + d, SIDE)
            remote(send.at[line(row)], here, ssem, rsem.at[y], (s, mine * SIDE + row)).start()

        @pl.when(mine != z)
        def _():
            remote(send.at[line(y)], here, ssem, rsem.at[y], (s, mine * SIDE + y)).start()

        @pl.when(mine == z)
        def _():
            pltpu.make_async_copy(send.at[line(y)], here, rsem.at[y]).start()

    def exchanged(send, ssem):
        @pl.when(mine != z)
        def _():
            wait_bytes(send, ssem)

        @pl.when(mine == z)
        def _():
            wait_bytes(send.at[pl.ds(0, 7 * LINE)], ssem)

    def share(recv, rsem, ssem, csem):
        def step(j, carry):
            half = (j + 1) // 2
            row = lax.rem(y + SIDE + jnp.where(lax.rem(j, 2) == 1, half, -half), SIDE)
            here = recv.at[line(mine * SIDE + row)]
            wait_bytes(here, rsem.at[row])
            for d in NEAR:
                remote(here, here, ssem, csem, along_seq(d)).start()
            return carry

        lax.fori_loop(0, SIDE, step, 0)

    def gather_lines(recv, ref):
        wide[: 64 * LINE] = recv[...].astype(F32)
        for t in range(TILES):
            ref[:, 128 * t : 128 * (t + 1)] = wide[pl.ds(t, 64, stride=LINE), :].astype(BF)

    fold(part, p_send)
    to_owners(p_send, p_recv, p_s, p_r)
    pl.semaphore_wait(ysem, 2)
    pl.semaphore_wait(zsem, 2)

    @pl.when(mine != z)
    def _():
        signal(wsem, (s, mine * SIDE + y))

    wait_bytes(st_recv.at[pl.ds(0, SEQ - 1)], st_r)
    tops = [st_recv[i][:, 0:1] for i in range(SEQ)]
    sums = [st_recv[i][:, 64:65] for i in range(SEQ)]
    peak = tops[0]
    for i in range(1, SEQ):
        peak = jnp.maximum(peak, tops[i])
    weights = [jnp.exp(tops[i] - peak) * sums[i] for i in range(SEQ)]
    norm = weights[0]
    for i in range(1, SEQ):
        norm = norm + weights[i]
    norm = 1.0 / norm

    @pl.when(mine != z)
    def _():
        pl.semaphore_wait(wsem, 1)

    wait_bytes(p_recv.at[pl.ds(0, SEQ - 1)], p_r)
    low = high = None
    for i in range(SEQ):
        got = p_recv[i].astype(F32)
        w = weights[i] * norm
        a, b = got[:SIDE] * w, got[SIDE:] * w
        low, high = (a, b) if low is None else (low + a, high + b)
    exchange(low, high, r1_send, c1_recv, b1_s, b1_r)
    for d in (4, 2, 6):
        remote(kb_send, kb_recv.at[core, x], kb_s, kb_r, along_seq(d)).start()
    share(c1_recv, b1_r, c1_s, c1_r)
    loads[2].wait()
    loads[3].wait()
    wait_bytes(c1_recv.at[pl.ds(0, 56 * LINE)], c1_r)

    gather_lines(c1_recv, xv)
    hidden = gelu(jnp.dot(xv[...], w1[...], preferred_element_type=F32)).astype(BF)
    fold(jnp.dot(hidden, w2[...], preferred_element_type=F32), q_send)
    to_owners(q_send, q_recv, q_s, q_r)
    wait_bytes(q_recv.at[pl.ds(0, SEQ - 1)], q_r)
    low = high = None
    for i in range(SEQ):
        got = q_recv[i].astype(F32)
        a, b = got[:SIDE], got[SIDE:]
        low, high = (a, b) if low is None else (low + a, high + b)
    exchange(low, high, r2_send, c2_recv, b2_s, b2_r)

    wait_bytes(kb_recv.at[0, pl.ds(0, 3)], kb_r)
    forward = remote(kb_recv.at[core], kb_recv.at[core], kf_s, kf_r, (s + 1 - 2 * core, e))
    forward.start()
    forward.wait()
    for src in range(SEQ):
        got = kb_recv[src % 2, src // 2]
        kfull[ROWS * src : ROWS * src + PACK, WINDOW:128] = got[:PACK, :WINDOW]
        kfull[ROWS * src + PACK : ROWS * (src + 1), WINDOW:128] = got[:PACK, WINDOW:]
        kfull[ROWS * src : ROWS * (src + 1), 128:] = got[PACK:]
    every = jnp.dot(tok[...], kfull[...], preferred_element_type=F32)
    up = jnp.exp(every - jnp.max(every, axis=1, keepdims=True))
    comb[...] = (up[:, :WINDOW] * (1.0 / jnp.sum(up, axis=1, keepdims=True))).astype(BF)

    share(c2_recv, b2_r, c2_s, c2_r)
    wait_bytes(ka_recv.at[pl.ds(0, SEQ - 1)], ka_s)
    wait_bytes(kb_recv.at[0, pl.ds(0, 3)], kb_s)
    wait_bytes(st_recv.at[pl.ds(0, SEQ - 1)], st_s)
    wait_bytes(p_recv.at[pl.ds(0, SEQ - 1)], p_s)
    wait_bytes(q_recv.at[pl.ds(0, SEQ - 1)], q_s)
    exchanged(r1_send, b1_s)
    exchanged(r2_send, b2_s)
    wait_bytes(c1_recv.at[pl.ds(0, 56 * LINE)], c1_s)

    wait_bytes(c2_recv.at[pl.ds(0, 56 * LINE)], c2_r)
    gather_lines(c2_recv, mixed_in)
    wait_bytes(c2_recv.at[pl.ds(0, 56 * LINE)], c2_s)


def mix_kernel(comb, rows, out_hbm, outv, sem):
    copies = []
    for c in range(5):
        cols = slice(256 * c, 256 * (c + 1))
        outv[:, cols] = jnp.dot(comb[...], rows[:, cols], preferred_element_type=F32).astype(BF)
        copies.append(pltpu.make_async_copy(outv.at[:, cols], out_hbm.at[0, :, cols], sem.at[c]))
        copies[-1].start()
    for copy in copies:
        copy.wait()


def on_device(tokens, slot_keys, expert_in, expert_out):
    dma = pltpu.SemaphoreType.DMA
    reg = pltpu.SemaphoreType.REGULAR
    vm = pltpu.VMEM
    lines, folded = (SIDE * LINE, 128), (SEQ, 16, HALF)
    scratch = [
        vm((PATCH, D), BF), vm((ROWS, SLOTS), BF), vm((D, HID), BF), vm((HID, D), BF),
        vm((PACK, 128), BF), vm((SEQ, PACK, 128), BF), vm((REST, 128), BF), vm((2, 4, REST, 128), BF), vm((D, SLOTS), BF),
        vm((WINDOW, 128), F32), vm((SEQ, SIDE, 128), F32), vm(folded, BF), vm(folded, BF), vm(folded, BF), vm(folded, BF),
        vm(((SIDE + 1) * LINE, 128), F32), vm((65 * LINE, 128), F32), vm(lines, BF), vm(lines, BF),
        vm((64 * LINE, 128), BF), vm((64 * LINE, 128), BF), vm((64, D), BF),
        dma((4,)), reg, reg, reg,
    ] + [dma] * 13 + [dma((SIDE,)), dma, dma((SIDE,))] + [dma] * 4
    operands = [pltpu.with_memory_space_constraint(a, pltpu.HBM) for a in (tokens, slot_keys, expert_in, expert_out)]
    in_vmem = pl.BlockSpec(memory_space=pltpu.VMEM)
    anywhere = pl.BlockSpec(memory_space=pl.ANY)
    comb, rows = pl.pallas_call(
        kernel,
        name="moe",
        out_shape=(jax.ShapeDtypeStruct((PATCH, WINDOW), BF), jax.ShapeDtypeStruct((64, D), BF)),
        in_specs=[anywhere] * 4,
        out_specs=(in_vmem, in_vmem),
        scratch_shapes=scratch,
        compiler_params=pltpu.CompilerParams(collective_id=0, has_side_effects=True, vmem_limit_bytes=48 * 1024 * 1024),
    )(*operands)
    return pl.pallas_call(
        mix_kernel,
        name="mix",
        out_shape=jax.ShapeDtypeStruct(tokens.shape, BF),
        in_specs=[in_vmem, in_vmem],
        out_specs=anywhere,
        scratch_shapes=[vm((PATCH, D), BF), dma((5,))],
        compiler_params=pltpu.CompilerParams(vmem_limit_bytes=48 * 1024 * 1024),
    )(comb, rows)


def solution(mesh):
    return jax.shard_map(
        on_device,
        mesh=mesh,
        in_specs=(
            P("exp", "seq", None),
            P("seq", None),
            P("exp", None, "seq"),
            P("exp", "seq", None),
        ),
        out_specs=P("exp", "seq", None),
        check_vma=False,
    )
```

```python
import jax
import jax.numpy as jnp
from jax import lax
from jax.experimental import pallas as pl
from jax.experimental.pallas import tpu as pltpu
from jax.sharding import PartitionSpec as P

MESH = pl.DeviceIdType.MESH
BF = jnp.bfloat16
F32 = jnp.float32
SEQ = 8
SIDE = 8
D = 1280
HID = 640
PATCH = 256
SLOTS = 256
WINDOW = 64
ROWS = D // SEQ
HALF = D // 2
PACK = ROWS // 2
REST = PACK + ROWS
LINE = 16
TILES = D // 128
NEAR = (4, 5, 3, 6, 2, 7, 1)


def wait_bytes(ref, sem):
    pltpu.make_async_copy(ref, ref, sem).wait()


def gelu(v):
    inner = 0.7978845608028654 * (v + 0.044715 * (v * v * v))
    return 0.5 * v * (1.0 + jnp.tanh(inner))


def kernel(
    tok_hbm, keys_hbm, w1_hbm, w2_hbm, comb, mixed_in,
    tok, keys, w1, w2,
    ka_send, ka_recv, kb_send, kb_recv, kfull,
    st_send, st_recv, p_send, p_recv, q_send, q_recv,
    stage, wide, r1_send, r2_send, c1_recv, c2_recv, xv,
    load_sem, ysem, rsem, zsem, wsem,
    ka_s, ka_r, kb_s, kb_r, kf_s, kf_r, st_s, st_r, p_s, p_r, q_s, q_r,
    b1_s, b1_r, b2_s, b2_r, c1_s, c1_r, c2_s, c2_r,
):
    s = lax.axis_index("seq")
    e = lax.axis_index("exp")
    x, core = s // 2, lax.rem(s, 2)
    z, y = e // SIDE, lax.rem(e, SIDE)
    mine = lax.rem(s - z + SIDE, SIDE)

    def along_y(d):
        return (s, z * SIDE + lax.rem(y + d, SIDE))

    def along_z(d):
        return (s, lax.rem(z + d, SIDE) * SIDE + y)

    def along_seq(d):
        return (lax.rem(s + d, SEQ), e)

    def signal(sem, device):
        pl.semaphore_signal(sem, inc=1, device_id=device, device_id_type=MESH)

    def remote(src, dst, ssem, rsem, device):
        return pltpu.make_async_remote_copy(
            src_ref=src, dst_ref=dst, send_sem=ssem, recv_sem=rsem, device_id=device, device_id_type=MESH
        )

    def group_of(d):
        return lax.rem(s + d - z + SIDE, SIDE)

    barrier = pltpu.get_barrier_semaphore()
    for d in NEAR:
        signal(barrier, along_seq(d))
    for d in (2, 6, 1, 7):
        signal(barrier, along_y(d))
        signal(barrier, along_z(d))
    loads = [
        pltpu.make_async_copy(keys_hbm, keys, load_sem.at[0]),
        pltpu.make_async_copy(tok_hbm.at[0], tok, load_sem.at[1]),
        pltpu.make_async_copy(w1_hbm.at[0], w1, load_sem.at[2]),
        pltpu.make_async_copy(w2_hbm.at[0], w2, load_sem.at[3]),
    ]
    for load in loads:
        load.start()
    stage[...] = jnp.zeros_like(stage)

    loads[0].wait()
    kk = keys[...]
    ka = jnp.concatenate([kk[:PACK, :WINDOW], kk[PACK:, :WINDOW]], axis=1)
    ka_send[...] = ka
    ka_recv[s] = ka
    kb_send[:PACK] = jnp.concatenate([kk[:PACK, WINDOW:128], kk[PACK:, WINDOW:128]], axis=1)
    kb_send[PACK:] = kk[:, 128:]
    kb_recv[core, x] = kb_send[...]
    pl.semaphore_wait(barrier, 15)
    for d in NEAR:
        remote(ka_send, ka_recv.at[s], ka_s, ka_r, along_seq(d)).start()
    for d in (2, 6, 1, 7):
        signal(ysem, along_y(d))
    for d in (2, 6):
        signal(zsem, along_z(d))
    pl.semaphore_wait(ysem, 4)
    for d in (2, 6):
        signal(rsem, along_y(d))
    loads[1].wait()
    wait_bytes(ka_recv.at[pl.ds(0, SEQ - 1)], ka_r)
    for src in range(SEQ):
        got = ka_recv[src]
        kfull[ROWS * src : ROWS * src + PACK, :WINDOW] = got[:, :WINDOW]
        kfull[ROWS * src + PACK : ROWS * (src + 1), :WINDOW] = got[:, WINDOW:]

    scores = jnp.dot(tok[...], kfull[:, :WINDOW], preferred_element_type=F32)
    scores_t = scores.T
    top = jnp.max(scores_t, axis=1, keepdims=True)
    raised = jnp.exp(scores_t - top)
    total = jnp.sum(raised, axis=1, keepdims=True)
    lane = lax.broadcasted_iota(jnp.int32, (WINDOW, 128), 1)
    st_send[...] = jnp.where(lane < 64, top, total)
    for d in NEAR:
        rows = pl.ds(pl.multiple_of(group_of(d) * SIDE, SIDE), SIDE)
        remote(st_send.at[rows], st_recv.at[s], st_s, st_r, along_seq(d)).start()
    st_recv[s] = st_send[pl.ds(pl.multiple_of(mine * SIDE, SIDE), SIDE)]
    pl.semaphore_wait(rsem, 2)
    pl.semaphore_wait(zsem, 2)

    @pl.when(mine != z)
    def _():
        signal(wsem, (s, mine * SIDE + y))

    part = jnp.dot(raised.astype(BF), tok[...], preferred_element_type=F32)
    part = part * (1.0 / total)

    def fold(values, ref):
        for g in range(SIDE):
            block = values[g * SIDE : (g + 1) * SIDE]
            ref[g] = jnp.concatenate([block[:, :HALF], block[:, HALF:]], axis=0).astype(BF)

    def to_owners(send, recv, ssem, rsem):
        for d in NEAR:
            remote(send.at[group_of(d)], recv.at[s], ssem, rsem, along_seq(d)).start()
        recv[s] = send[mine]

    def line(row):
        return pl.ds(pl.multiple_of(row * LINE, LINE), LINE)

    def exchange(low, high, send, recv, ssem, rsem):
        for t in range(TILES):
            half = low if t < TILES // 2 else high
            c = (t % (TILES // 2)) * 128
            stage[pl.ds(t, SIDE, stride=LINE), :] = half[:, c : c + 128]
        send[...] = stage[: SIDE * LINE].astype(BF)
        here = recv.at[lax.rem(z, 2), line((z // 2) * SIDE + y)]
        for d in NEAR:
            row = lax.rem(y + d, SIDE)
            for dx in (2, 1, 3, 0):
                to = (lax.rem(x + dx, 4) * 2 + core, mine * SIDE + row)
                remote(send.at[line(row)], here, ssem, rsem, to).start()
        for dx in (2, 1, 3):
            to = (lax.rem(x + dx, 4) * 2 + core, mine * SIDE + y)
            remote(send.at[line(y)], here, ssem, rsem, to).start()

        @pl.when(mine != z)
        def _():
            remote(send.at[line(y)], here, ssem, rsem, (s, mine * SIDE + y)).start()

        @pl.when(mine == z)
        def _():
            pltpu.make_async_copy(send.at[line(y)], here, rsem).start()

    def exchanged(recv, ssem):
        @pl.when(mine != z)
        def _():
            wait_bytes(recv.at[0], ssem)

        @pl.when(mine == z)
        def _():
            wait_bytes(recv.at[0, pl.ds(0, 31 * LINE)], ssem)

    def share(recv, rsem, ssem, csem):
        own = lax.rem(core + z, 2)
        wait_bytes(recv.at[own], rsem)
        remote(recv.at[own], recv.at[own], ssem, csem, (s + 1 - 2 * core, e)).start()
        wide[pl.ds(pl.multiple_of(own * 32 * LINE, 32 * LINE), 32 * LINE)] = recv[own].astype(F32)
        other = 1 - own
        wait_bytes(recv.at[other], csem)
        wide[pl.ds(pl.multiple_of(other * 32 * LINE, 32 * LINE), 32 * LINE)] = recv[other].astype(F32)

    def gather_lines(ref):
        for t in range(TILES):
            tile = wide[pl.ds(t, 64, stride=LINE), :]
            groups = [tile[SIDE * ((g % 2) * 4 + g // 2) :][:SIDE] for g in range(SIDE)]
            ref[:, 128 * t : 128 * (t + 1)] = jnp.concatenate(groups, axis=0).astype(BF)

    fold(part, p_send)
    to_owners(p_send, p_recv, p_s, p_r)

    wait_bytes(st_recv.at[pl.ds(0, SEQ - 1)], st_r)
    tops = [st_recv[i][:, 0:1] for i in range(SEQ)]
    sums = [st_recv[i][:, 64:65] for i in range(SEQ)]
    peak = tops[0]
    for i in range(1, SEQ):
        peak = jnp.maximum(peak, tops[i])
    weights = [jnp.exp(tops[i] - peak) * sums[i] for i in range(SEQ)]
    norm = weights[0]
    for i in range(1, SEQ):
        norm = norm + weights[i]
    norm = 1.0 / norm

    @pl.when(mine != z)
    def _():
        pl.semaphore_wait(wsem, 1)

    wait_bytes(p_recv.at[pl.ds(0, SEQ - 1)], p_r)
    low = high = None
    for i in range(SEQ):
        got = p_recv[i].astype(F32)
        w = weights[i] * norm
        a, b = got[:SIDE] * w, got[SIDE:] * w
        low, high = (a, b) if low is None else (low + a, high + b)
    exchange(low, high, r1_send, c1_recv, b1_s, b1_r)
    for d in (4, 2, 6):
        remote(kb_send, kb_recv.at[core, x], kb_s, kb_r, along_seq(d)).start()
    loads[2].wait()
    loads[3].wait()
    share(c1_recv, b1_r, c1_s, c1_r)

    gather_lines(xv)
    hidden = gelu(jnp.dot(xv[...], w1[...], preferred_element_type=F32)).astype(BF)
    fold(jnp.dot(hidden, w2[...], preferred_element_type=F32), q_send)
    to_owners(q_send, q_recv, q_s, q_r)
    wait_bytes(q_recv.at[pl.ds(0, SEQ - 1)], q_r)
    low = high = None
    for i in range(SEQ):
        got = q_recv[i].astype(F32)
        a, b = got[:SIDE], got[SIDE:]
        low, high = (a, b) if low is None else (low + a, high + b)
    exchange(low, high, r2_send, c2_recv, b2_s, b2_r)

    wait_bytes(kb_recv.at[0, pl.ds(0, 3)], kb_r)
    forward = remote(kb_recv.at[core], kb_recv.at[core], kf_s, kf_r, (s + 1 - 2 * core, e))
    forward.start()
    forward.wait()
    for src in range(SEQ):
        got = kb_recv[src % 2, src // 2]
        kfull[ROWS * src : ROWS * src + PACK, WINDOW:128] = got[:PACK, :WINDOW]
        kfull[ROWS * src + PACK : ROWS * (src + 1), WINDOW:128] = got[:PACK, WINDOW:]
        kfull[ROWS * src : ROWS * (src + 1), 128:] = got[PACK:]
    every = jnp.dot(tok[...], kfull[...], preferred_element_type=F32)
    up = jnp.exp(every - jnp.max(every, axis=1, keepdims=True))
    comb[...] = (up[:, :WINDOW] * (1.0 / jnp.sum(up, axis=1, keepdims=True))).astype(BF)

    wait_bytes(ka_recv.at[pl.ds(0, SEQ - 1)], ka_s)
    wait_bytes(kb_recv.at[0, pl.ds(0, 3)], kb_s)
    wait_bytes(st_recv.at[pl.ds(0, SEQ - 1)], st_s)
    wait_bytes(p_recv.at[pl.ds(0, SEQ - 1)], p_s)
    wait_bytes(q_recv.at[pl.ds(0, SEQ - 1)], q_s)
    exchanged(c1_recv, b1_s)
    wait_bytes(c1_recv.at[0], c1_s)
    share(c2_recv, b2_r, c2_s, c2_r)
    gather_lines(mixed_in)
    exchanged(c2_recv, b2_s)
    wait_bytes(c2_recv.at[0], c2_s)


def mix_kernel(comb, rows, out_hbm, outv, sem):
    copies = []
    for c in range(5):
        cols = slice(256 * c, 256 * (c + 1))
        outv[:, cols] = jnp.dot(comb[...], rows[:, cols], preferred_element_type=F32).astype(BF)
        copies.append(pltpu.make_async_copy(outv.at[:, cols], out_hbm.at[0, :, cols], sem.at[c]))
        copies[-1].start()
    for copy in copies:
        copy.wait()


def on_device(tokens, slot_keys, expert_in, expert_out):
    dma = pltpu.SemaphoreType.DMA
    reg = pltpu.SemaphoreType.REGULAR
    vm = pltpu.VMEM
    lines, folded = (SIDE * LINE, 128), (SEQ, 16, HALF)
    scratch = [
        vm((PATCH, D), BF), vm((ROWS, SLOTS), BF), vm((D, HID), BF), vm((HID, D), BF),
        vm((PACK, 128), BF), vm((SEQ, PACK, 128), BF), vm((REST, 128), BF), vm((2, 4, REST, 128), BF), vm((D, SLOTS), BF),
        vm((WINDOW, 128), F32), vm((SEQ, SIDE, 128), F32), vm(folded, BF), vm(folded, BF), vm(folded, BF), vm(folded, BF),
        vm(((SIDE + 1) * LINE, 128), F32), vm((65 * LINE, 128), F32), vm(lines, BF), vm(lines, BF),
        vm((2, 32 * LINE, 128), BF), vm((2, 32 * LINE, 128), BF), vm((64, D), BF),
        dma((4,)), reg, reg, reg, reg,
    ] + [dma] * 20
    operands = [pltpu.with_memory_space_constraint(a, pltpu.HBM) for a in (tokens, slot_keys, expert_in, expert_out)]
    in_vmem = pl.BlockSpec(memory_space=pltpu.VMEM)
    anywhere = pl.BlockSpec(memory_space=pl.ANY)
    comb, rows = pl.pallas_call(
        kernel,
        name="moe",
        out_shape=(jax.ShapeDtypeStruct((PATCH, WINDOW), BF), jax.ShapeDtypeStruct((64, D), BF)),
        in_specs=[anywhere] * 4,
        out_specs=(in_vmem, in_vmem),
        scratch_shapes=scratch,
        compiler_params=pltpu.CompilerParams(collective_id=0, has_side_effects=True, vmem_limit_bytes=48 * 1024 * 1024),
    )(*operands)
    return pl.pallas_call(
        mix_kernel,
        name="mix",
        out_shape=jax.ShapeDtypeStruct(tokens.shape, BF),
        in_specs=[in_vmem, in_vmem],
        out_specs=anywhere,
        scratch_shapes=[vm((PATCH, D), BF), dma((5,))],
        compiler_params=pltpu.CompilerParams(vmem_limit_bytes=48 * 1024 * 1024),
    )(comb, rows)


def solution(mesh):
    return jax.shard_map(
        on_device,
        mesh=mesh,
        in_specs=(
            P("exp", "seq", None),
            P("seq", None),
            P("exp", None, "seq"),
            P("exp", "seq", None),
        ),
        out_specs=P("exp", "seq", None),
        check_vma=False,
    )
```

```python
import jax
import jax.numpy as jnp
from jax import lax
from jax.experimental import pallas as pl
from jax.experimental.pallas import tpu as pltpu
from jax.sharding import PartitionSpec as P

MESH = pl.DeviceIdType.MESH
BF = jnp.bfloat16
F32 = jnp.float32
SEQ = 8
SIDE = 8
D = 1280
HID = 640
PATCH = 256
SLOTS = 256
WINDOW = 64
ROWS = D // SEQ
HALF = D // 2
PACK = ROWS // 2
REST = PACK + ROWS
LINE = 16
TILES = D // 128
NEAR = (4, 5, 3, 6, 2, 7, 1)


def wait_bytes(ref, sem):
    pltpu.make_async_copy(ref, ref, sem).wait()


def gelu(v):
    inner = 0.7978845608028654 * (v + 0.044715 * (v * v * v))
    return 0.5 * v * (1.0 + jnp.tanh(inner))


def kernel(
    tok_hbm, keys_hbm, w1_hbm, w2_hbm, comb, mixed_in,
    tok, keys, w1, w2,
    ka_send, ka_recv, kb_send, kb_recv, kfull,
    st_send, st_recv, p_send, p_recv, q_send, q_recv,
    stage, r1_send, r2_send, b1_recv, b2_recv, c1_recv, c2_recv, flat, xv,
    load_sem, ysem, zsem, wsem,
    ka_s, ka_r, kb_s, kb_r, kf_s, kf_r, st_s, st_r, p_s, p_r, q_s, q_r,
    b1_s, b1_r, b2_s, b2_r, c1_s, c1_r, c2_s, c2_r,
):
    s = lax.axis_index("seq")
    e = lax.axis_index("exp")
    x, core = s // 2, lax.rem(s, 2)
    z, y = e // SIDE, lax.rem(e, SIDE)
    mine = lax.rem(s - z + SIDE, SIDE)

    def along_y(d):
        return (s, z * SIDE + lax.rem(y + d, SIDE))

    def along_z(d):
        return (s, lax.rem(z + d, SIDE) * SIDE + y)

    def along_seq(d):
        return (lax.rem(s + d, SEQ), e)

    def signal(sem, device):
        pl.semaphore_signal(sem, inc=1, device_id=device, device_id_type=MESH)

    def remote(src, dst, ssem, rsem, device):
        return pltpu.make_async_remote_copy(
            src_ref=src, dst_ref=dst, send_sem=ssem, recv_sem=rsem, device_id=device, device_id_type=MESH
        )

    def group_of(peer):
        return lax.rem(peer - z + SIDE, SIDE)

    near_first = [s + 1 - 2 * core] + [lax.rem(x + dx, 4) * 2 + c for dx in (1, 3, 2) for c in range(2)]
    far_first = near_first[::-1]

    loads = [
        pltpu.make_async_copy(keys_hbm, keys, load_sem.at[0]),
        pltpu.make_async_copy(tok_hbm.at[0], tok, load_sem.at[1]),
        pltpu.make_async_copy(w1_hbm.at[0], w1, load_sem.at[2]),
        pltpu.make_async_copy(w2_hbm.at[0], w2, load_sem.at[3]),
    ]
    loads[0].start()
    barrier = pltpu.get_barrier_semaphore()
    for peer in far_first:
        signal(barrier, (peer, e))
    for d in (2, 6, 1, 7):
        signal(barrier, along_y(d))
        signal(barrier, along_z(d))
    for load in loads[1:]:
        load.start()
    stage[...] = jnp.zeros_like(stage)

    loads[0].wait()
    kk = keys[...]
    ka = jnp.concatenate([kk[:PACK, :WINDOW], kk[PACK:, :WINDOW]], axis=1)
    ka_send[...] = ka
    ka_recv[s] = ka
    kb_send[:PACK] = jnp.concatenate([kk[:PACK, WINDOW:128], kk[PACK:, WINDOW:128]], axis=1)
    kb_send[PACK:] = kk[:, 128:]
    kb_recv[core, x] = kb_send[...]
    pl.semaphore_wait(barrier, 15)
    for peer in far_first:
        remote(ka_send, ka_recv.at[s], ka_s, ka_r.at[s], (peer, e)).start()
    for d in (2, 6):
        signal(ysem, along_y(d))
        signal(zsem, along_z(d))
    loads[1].wait()
    for src in [s] + near_first:
        if src is not s:
            wait_bytes(ka_recv.at[src], ka_r.at[src])
        got = ka_recv[src]
        at = pl.multiple_of(src * ROWS, 16)
        kfull[pl.ds(at, PACK), :WINDOW] = got[:, :WINDOW]
        kfull[pl.ds(at + PACK, PACK), :WINDOW] = got[:, WINDOW:]

    scores = jnp.dot(tok[...], kfull[:, :WINDOW], preferred_element_type=F32)
    scores_t = scores.T
    top = jnp.max(scores_t, axis=1, keepdims=True)
    raised = jnp.exp(scores_t - top)
    total = jnp.sum(raised, axis=1, keepdims=True)
    lane = lax.broadcasted_iota(jnp.int32, (WINDOW, 128), 1)
    st_send[...] = jnp.where(lane < 64, top, total)
    for peer in far_first:
        rows = pl.ds(pl.multiple_of(group_of(peer) * SIDE, SIDE), SIDE)
        remote(st_send.at[rows], st_recv.at[s], st_s, st_r, (peer, e)).start()
    st_recv[s] = st_send[pl.ds(pl.multiple_of(mine * SIDE, SIDE), SIDE)]
    part = jnp.dot(raised.astype(BF), tok[...], preferred_element_type=F32)
    part = part * (1.0 / total)

    def fold(values, ref):
        for g in range(SIDE):
            block = values[g * SIDE : (g + 1) * SIDE]
            ref[g] = jnp.concatenate([block[:, :HALF], block[:, HALF:]], axis=0).astype(BF)

    def to_owners(send, recv, ssem, rsem):
        for peer in far_first:
            remote(send.at[group_of(peer)], recv.at[s], ssem, rsem.at[s], (peer, e)).start()

    def owners_sum(send, recv, rsem, weight):
        low = high = None
        for src in [s] + near_first:
            if src is s:
                got = send[mine].astype(F32)
            else:
                wait_bytes(recv.at[src], rsem.at[src])
                got = recv[src].astype(F32)
            a, b = got[:SIDE], got[SIDE:]
            if weight is not None:
                w = weight(src)
                a, b = a * w, b * w
            low, high = (a, b) if low is None else (low + a, high + b)
        return low, high

    def exchange(low, high, send, recv, ssem, rsem):
        for t in range(TILES):
            half = low if t < TILES // 2 else high
            c = (t % (TILES // 2)) * 128
            stage[pl.ds(t, SIDE, stride=LINE), :] = half[:, c : c + 128]
        send[...] = stage[: SIDE * LINE].astype(BF)
        here = recv.at[pl.ds(pl.multiple_of(y * LINE, LINE), LINE)]
        for d in NEAR:
            row = lax.rem(y + d, SIDE)
            src = send.at[pl.ds(pl.multiple_of(row * LINE, LINE), LINE)]
            remote(src, here, ssem, rsem, (s, mine * SIDE + row)).start()
        src = send.at[pl.ds(pl.multiple_of(y * LINE, LINE), LINE)]

        @pl.when(mine != z)
        def _():
            remote(src, here, ssem, rsem, (s, mine * SIDE + y)).start()

        @pl.when(mine == z)
        def _():
            pltpu.make_async_copy(src, here, rsem).start()

    def exchanged(recv, ssem):
        @pl.when(mine != z)
        def _():
            wait_bytes(recv, ssem)

        @pl.when(mine == z)
        def _():
            wait_bytes(recv.at[pl.ds(0, 7 * LINE)], ssem)

    def share(lines, recv, ssem, rsem):
        stage[: SIDE * LINE] = lines[...].astype(F32)
        parts = [stage[pl.ds(t, SIDE, stride=LINE), :] for t in range(TILES)]
        low = jnp.concatenate(parts[: TILES // 2], axis=1)
        high = jnp.concatenate(parts[TILES // 2 :], axis=1)
        recv[s] = jnp.concatenate([low, high], axis=0).astype(BF)
        for peer in far_first:
            remote(recv.at[s], recv.at[s], ssem, rsem.at[s], (peer, e)).start()

    def unfold(recv, rsem, ref):
        for src in [s] + near_first:
            if src is not s:
                wait_bytes(recv.at[src], rsem.at[src])
            got = recv[src].astype(F32)
            rows = pl.ds(pl.multiple_of(group_of(src) * SIDE, SIDE), SIDE)
            flat[rows, :HALF] = got[:SIDE]
            flat[rows, HALF:] = got[SIDE:]
        ref[...] = flat[...].astype(BF)

    fold(part, p_send)
    to_owners(p_send, p_recv, p_s, p_r)
    pl.semaphore_wait(ysem, 2)
    pl.semaphore_wait(zsem, 2)

    @pl.when(mine != z)
    def _():
        signal(wsem, (s, mine * SIDE + y))

    wait_bytes(st_recv.at[pl.ds(0, SEQ - 1)], st_r)
    tops = [st_recv[i][:, 0:1] for i in range(SEQ)]
    sums = [st_recv[i][:, 64:65] for i in range(SEQ)]
    peak = tops[0]
    for i in range(1, SEQ):
        peak = jnp.maximum(peak, tops[i])
    weights = [jnp.exp(tops[i] - peak) * sums[i] for i in range(SEQ)]
    norm = weights[0]
    for i in range(1, SEQ):
        norm = norm + weights[i]
    norm = 1.0 / norm

    @pl.when(mine != z)
    def _():
        pl.semaphore_wait(wsem, 1)

    low, high = owners_sum(p_send, p_recv, p_r, lambda i: jnp.exp(st_recv[i][:, 0:1] - peak) * st_recv[i][:, 64:65] * norm)
    exchange(low, high, r1_send, b1_recv, b1_s, b1_r)
    for d in (4, 2, 6):
        remote(kb_send, kb_recv.at[core, x], kb_s, kb_r, along_seq(d)).start()
    wait_bytes(b1_recv, b1_r)
    share(b1_recv, c1_recv, c1_s, c1_r)
    loads[2].wait()
    loads[3].wait()

    unfold(c1_recv, c1_r, xv)
    hidden = gelu(jnp.dot(xv[...], w1[...], preferred_element_type=F32)).astype(BF)
    fold(jnp.dot(hidden, w2[...], preferred_element_type=F32), q_send)
    to_owners(q_send, q_recv, q_s, q_r)
    low, high = owners_sum(q_send, q_recv, q_r, None)
    exchange(low, high, r2_send, b2_recv, b2_s, b2_r)

    wait_bytes(kb_recv.at[0, pl.ds(0, 3)], kb_r)
    forward = remote(kb_recv.at[core], kb_recv.at[core], kf_s, kf_r, (s + 1 - 2 * core, e))
    forward.start()
    forward.wait()
    for src in range(SEQ):
        got = kb_recv[src % 2, src // 2]
        kfull[ROWS * src : ROWS * src + PACK, WINDOW:128] = got[:PACK, :WINDOW]
        kfull[ROWS * src + PACK : ROWS * (src + 1), WINDOW:128] = got[:PACK, WINDOW:]
        kfull[ROWS * src : ROWS * (src + 1), 128:] = got[PACK:]
    every = jnp.dot(tok[...], kfull[...], preferred_element_type=F32)
    up = jnp.exp(every - jnp.max(every, axis=1, keepdims=True))
    comb[...] = (up[:, :WINDOW] * (1.0 / jnp.sum(up, axis=1, keepdims=True))).astype(BF)

    wait_bytes(b2_recv, b2_r)
    share(b2_recv, c2_recv, c2_s, c2_r)
    wait_bytes(ka_recv.at[pl.ds(0, SEQ - 1)], ka_s)
    wait_bytes(kb_recv.at[0, pl.ds(0, 3)], kb_s)
    wait_bytes(st_recv.at[pl.ds(0, SEQ - 1)], st_s)
    wait_bytes(p_recv.at[pl.ds(0, SEQ - 1)], p_s)
    wait_bytes(q_recv.at[pl.ds(0, SEQ - 1)], q_s)
    exchanged(b1_recv, b1_s)
    exchanged(b2_recv, b2_s)
    wait_bytes(c1_recv.at[pl.ds(0, SEQ - 1)], c1_s)

    unfold(c2_recv, c2_r, mixed_in)
    wait_bytes(c2_recv.at[pl.ds(0, SEQ - 1)], c2_s)


def mix_kernel(comb, rows, out_hbm, outv, sem):
    copies = []
    for c in range(5):
        cols = slice(256 * c, 256 * (c + 1))
        outv[:, cols] = jnp.dot(comb[...], rows[:, cols], preferred_element_type=F32).astype(BF)
        copies.append(pltpu.make_async_copy(outv.at[:, cols], out_hbm.at[0, :, cols], sem.at[c]))
        copies[-1].start()
    for copy in copies:
        copy.wait()


def on_device(tokens, slot_keys, expert_in, expert_out):
    dma = pltpu.SemaphoreType.DMA
    reg = pltpu.SemaphoreType.REGULAR
    vm = pltpu.VMEM
    lines, folded = (SIDE * LINE, 128), (SEQ, 16, HALF)
    scratch = [
        vm((PATCH, D), BF), vm((ROWS, SLOTS), BF), vm((D, HID), BF), vm((HID, D), BF),
        vm((PACK, 128), BF), vm((SEQ, PACK, 128), BF), vm((REST, 128), BF), vm((2, 4, REST, 128), BF), vm((D, SLOTS), BF),
        vm((WINDOW, 128), F32), vm((SEQ, SIDE, 128), F32), vm(folded, BF), vm(folded, BF), vm(folded, BF), vm(folded, BF),
        vm(((SIDE + 1) * LINE, 128), F32), vm(lines, BF), vm(lines, BF), vm(lines, BF), vm(lines, BF),
        vm(folded, BF), vm(folded, BF), vm((64, D), F32), vm((64, D), BF),
        dma((4,)), reg, reg, reg,
        dma, dma((SEQ,)), dma, dma, dma, dma, dma, dma, dma, dma((SEQ,)), dma, dma((SEQ,)),
        dma, dma, dma, dma, dma, dma((SEQ,)), dma, dma((SEQ,)),
    ]
    operands = [pltpu.with_memory_space_constraint(a, pltpu.HBM) for a in (tokens, slot_keys, expert_in, expert_out)]
    in_vmem = pl.BlockSpec(memory_space=pltpu.VMEM)
    anywhere = pl.BlockSpec(memory_space=pl.ANY)
    comb, rows = pl.pallas_call(
        kernel,
        name="moe",
        out_shape=(jax.ShapeDtypeStruct((PATCH, WINDOW), BF), jax.ShapeDtypeStruct((64, D), BF)),
        in_specs=[anywhere] * 4,
        out_specs=(in_vmem, in_vmem),
        scratch_shapes=scratch,
        compiler_params=pltpu.CompilerParams(collective_id=0, has_side_effects=True, vmem_limit_bytes=48 * 1024 * 1024),
    )(*operands)
    return pl.pallas_call(
        mix_kernel,
        name="mix",
        out_shape=jax.ShapeDtypeStruct(tokens.shape, BF),
        in_specs=[in_vmem, in_vmem],
        out_specs=anywhere,
        scratch_shapes=[vm((PATCH, D), BF), dma((5,))],
        compiler_params=pltpu.CompilerParams(vmem_limit_bytes=48 * 1024 * 1024),
    )(comb, rows)


def solution(mesh):
    return jax.shard_map(
        on_device,
        mesh=mesh,
        in_specs=(
            P("exp", "seq", None),
            P("seq", None),
            P("exp", None, "seq"),
            P("exp", "seq", None),
        ),
        out_specs=P("exp", "seq", None),
        check_vma=False,
    )
```

```python
import jax
import jax.numpy as jnp
from jax import lax
from jax.experimental import pallas as pl
from jax.experimental.pallas import tpu as pltpu
from jax.sharding import PartitionSpec as P

MESH = pl.DeviceIdType.MESH
BF = jnp.bfloat16
F32 = jnp.float32
SEQ = 8
SIDE = 8
D = 1280
HID = 640
PATCH = 256
SLOTS = 256
WINDOW = 64
ROWS = D // SEQ
HALF = D // 2
PACK = ROWS // 2
REST = PACK + ROWS
LINE = 16
TILES = D // 128
NEAR = (4, 5, 3, 6, 2, 7, 1)


def wait_bytes(ref, sem):
    pltpu.make_async_copy(ref, ref, sem).wait()


def gelu(v):
    inner = 0.7978845608028654 * (v + 0.044715 * (v * v * v))
    return 0.5 * v * (1.0 + jnp.tanh(inner))


def kernel(
    tok_hbm, keys_hbm, w1_hbm, w2_hbm, comb, mixed_in,
    tok, keys, w1, w2,
    ka_send, ka_recv, kb_send, kb_recv, kfull,
    st_send, st_recv, p_send, p_recv, q_send, q_recv,
    stage, wide, r1_send, r2_send, c1_recv, c2_recv, xv,
    load_sem, ysem, rsem, zsem, wsem,
    ka_s, ka_r, kb_s, kb_r, kf_s, kf_r, st_s, st_r, p_s, p_r, q_s, q_r,
    b1_s, b1_r, b2_s, b2_r, c1_s, c1_r, c2_s, c2_r,
):
    s = lax.axis_index("seq")
    e = lax.axis_index("exp")
    x, core = s // 2, lax.rem(s, 2)
    z, y = e // SIDE, lax.rem(e, SIDE)
    skew = lax.rem(z + y, SIDE)
    mine = lax.rem(s - skew + SIDE, SIDE)

    def along_y(d):
        return (s, z * SIDE + lax.rem(y + d, SIDE))

    def along_z(d):
        return (s, lax.rem(z + d, SIDE) * SIDE + y)

    def along_seq(d):
        return (lax.rem(s + d, SEQ), e)

    def signal(sem, device):
        pl.semaphore_signal(sem, inc=1, device_id=device, device_id_type=MESH)

    def remote(src, dst, ssem, rsem, device):
        return pltpu.make_async_remote_copy(
            src_ref=src, dst_ref=dst, send_sem=ssem, recv_sem=rsem, device_id=device, device_id_type=MESH
        )

    def group_of(d):
        return lax.rem(s + d - skew + SIDE, SIDE)

    loads = [
        pltpu.make_async_copy(keys_hbm, keys, load_sem.at[0]),
        pltpu.make_async_copy(tok_hbm.at[0], tok, load_sem.at[1]),
        pltpu.make_async_copy(w1_hbm.at[0], w1, load_sem.at[2]),
        pltpu.make_async_copy(w2_hbm.at[0], w2, load_sem.at[3]),
    ]
    loads[0].start()
    barrier = pltpu.get_barrier_semaphore()
    for d in NEAR:
        signal(barrier, along_seq(d))
    for d in (2, 6, 1, 7):
        signal(barrier, along_y(d))
        signal(barrier, along_z(d))
    for load in loads[1:]:
        load.start()
    stage[...] = jnp.zeros_like(stage)

    loads[0].wait()
    kk = keys[...]
    ka = jnp.concatenate([kk[:PACK, :WINDOW], kk[PACK:, :WINDOW]], axis=1)
    ka_send[...] = ka
    ka_recv[s] = ka
    kb_send[:PACK] = jnp.concatenate([kk[:PACK, WINDOW:128], kk[PACK:, WINDOW:128]], axis=1)
    kb_send[PACK:] = kk[:, 128:]
    kb_recv[core, x] = kb_send[...]
    pl.semaphore_wait(barrier, 15)
    for d in NEAR:
        remote(ka_send, ka_recv.at[s], ka_s, ka_r, along_seq(d)).start()
    for d in (2, 6, 1, 7):
        signal(ysem, along_y(d))
    for d in (2, 6):
        signal(zsem, along_z(d))
    pl.semaphore_wait(ysem, 4)
    for d in (2, 6):
        signal(rsem, along_y(d))
    loads[1].wait()
    wait_bytes(ka_recv.at[pl.ds(0, SEQ - 1)], ka_r)
    for src in range(SEQ):
        got = ka_recv[src]
        kfull[ROWS * src : ROWS * src + PACK, :WINDOW] = got[:, :WINDOW]
        kfull[ROWS * src + PACK : ROWS * (src + 1), :WINDOW] = got[:, WINDOW:]

    scores = jnp.dot(tok[...], kfull[:, :WINDOW], preferred_element_type=F32)
    scores_t = scores.T
    place = lax.rem(lax.broadcasted_iota(jnp.int32, (SIDE, PATCH), 0), SIDE)
    groups = []
    for g in range(SIDE):
        block = scores_t[g * SIDE : (g + 1) * SIDE]
        for yk in range(1, SIDE):
            zk = (g - yk) % SIDE
            block = jnp.where(place == yk, scores_t[zk * SIDE : (zk + 1) * SIDE], block)
        groups.append(block)
    scores_t = jnp.concatenate(groups, axis=0)
    top = jnp.max(scores_t, axis=1, keepdims=True)
    raised = jnp.exp(scores_t - top)
    total = jnp.sum(raised, axis=1, keepdims=True)
    lane = lax.broadcasted_iota(jnp.int32, (WINDOW, 128), 1)
    st_send[...] = jnp.where(lane < 64, top, total)
    for d in NEAR:
        rows = pl.ds(pl.multiple_of(group_of(d) * SIDE, SIDE), SIDE)
        remote(st_send.at[rows], st_recv.at[s], st_s, st_r, along_seq(d)).start()
    st_recv[s] = st_send[pl.ds(pl.multiple_of(mine * SIDE, SIDE), SIDE)]
    pl.semaphore_wait(rsem, 2)
    pl.semaphore_wait(zsem, 2)
    for d in NEAR:
        signal(wsem, along_z(d))

    part = jnp.dot(raised.astype(BF), tok[...], preferred_element_type=F32)
    part = part * (1.0 / total)

    def fold(values, ref):
        for g in range(SIDE):
            block = values[g * SIDE : (g + 1) * SIDE]
            ref[g] = jnp.concatenate([block[:, :HALF], block[:, HALF:]], axis=0).astype(BF)

    def to_owners(send, recv, ssem, rsem):
        for d in NEAR:
            remote(send.at[group_of(d)], recv.at[s], ssem, rsem, along_seq(d)).start()
        recv[s] = send[mine]

    def line(row):
        return pl.ds(pl.multiple_of(row * LINE, LINE), LINE)

    def exchange(low, high, send, recv, ssem, rsem):
        for t in range(TILES):
            half = low if t < TILES // 2 else high
            c = (t % (TILES // 2)) * 128
            stage[pl.ds(t, SIDE, stride=LINE), :] = half[:, c : c + 128]
        send[...] = stage[: SIDE * LINE].astype(BF)
        here = recv.at[lax.rem(skew, 2), line((skew // 2) * SIDE + y)]
        for d in NEAR + (0,):
            row = lax.rem(y + d, SIDE)
            place = lax.rem(mine - row + SIDE, SIDE) * SIDE + row
            for dx in (2, 1, 3, 0):
                if d or dx:
                    to = (lax.rem(x + dx, 4) * 2 + core, place)
                    remote(send.at[line(row)], here, ssem, rsem, to).start()

        @pl.when(mine != skew)
        def _():
            remote(send.at[line(y)], here, ssem, rsem, (s, lax.rem(mine - y + SIDE, SIDE) * SIDE + y)).start()

        @pl.when(mine == skew)
        def _():
            pltpu.make_async_copy(send.at[line(y)], here, rsem).start()

    def exchanged(recv, ssem):
        @pl.when(mine != skew)
        def _():
            wait_bytes(recv.at[0], ssem)

        @pl.when(mine == skew)
        def _():
            wait_bytes(recv.at[0, pl.ds(0, 31 * LINE)], ssem)

    def share(recv, rsem, ssem, csem):
        own = lax.rem(core + skew, 2)
        wait_bytes(recv.at[own], rsem)
        remote(recv.at[own], recv.at[own], ssem, csem, (s + 1 - 2 * core, e)).start()
        wide[pl.ds(pl.multiple_of(own * 32 * LINE, 32 * LINE), 32 * LINE)] = recv[own].astype(F32)
        other = 1 - own
        wait_bytes(recv.at[other], csem)
        wide[pl.ds(pl.multiple_of(other * 32 * LINE, 32 * LINE), 32 * LINE)] = recv[other].astype(F32)

    def gather_lines(ref):
        for t in range(TILES):
            tile = wide[pl.ds(t, 64, stride=LINE), :]
            groups = [tile[SIDE * ((g % 2) * 4 + g // 2) :][:SIDE] for g in range(SIDE)]
            ref[:, 128 * t : 128 * (t + 1)] = jnp.concatenate(groups, axis=0).astype(BF)

    fold(part, p_send)
    to_owners(p_send, p_recv, p_s, p_r)

    wait_bytes(st_recv.at[pl.ds(0, SEQ - 1)], st_r)
    tops = [st_recv[i][:, 0:1] for i in range(SEQ)]
    sums = [st_recv[i][:, 64:65] for i in range(SEQ)]
    peak = tops[0]
    for i in range(1, SEQ):
        peak = jnp.maximum(peak, tops[i])
    weights = [jnp.exp(tops[i] - peak) * sums[i] for i in range(SEQ)]
    norm = weights[0]
    for i in range(1, SEQ):
        norm = norm + weights[i]
    norm = 1.0 / norm

    pl.semaphore_wait(wsem, 7)
    wait_bytes(p_recv.at[pl.ds(0, SEQ - 1)], p_r)
    low = high = None
    for i in range(SEQ):
        got = p_recv[i].astype(F32)
        w = weights[i] * norm
        a, b = got[:SIDE] * w, got[SIDE:] * w
        low, high = (a, b) if low is None else (low + a, high + b)
    exchange(low, high, r1_send, c1_recv, b1_s, b1_r)
    for d in (4, 2, 6):
        remote(kb_send, kb_recv.at[core, x], kb_s, kb_r, along_seq(d)).start()
    loads[2].wait()
    loads[3].wait()
    share(c1_recv, b1_r, c1_s, c1_r)

    gather_lines(xv)
    hidden = gelu(jnp.dot(xv[...], w1[...], preferred_element_type=F32)).astype(BF)
    fold(jnp.dot(hidden, w2[...], preferred_element_type=F32), q_send)
    to_owners(q_send, q_recv, q_s, q_r)
    wait_bytes(q_recv.at[pl.ds(0, SEQ - 1)], q_r)
    low = high = None
    for i in range(SEQ):
        got = q_recv[i].astype(F32)
        a, b = got[:SIDE], got[SIDE:]
        low, high = (a, b) if low is None else (low + a, high + b)
    exchange(low, high, r2_send, c2_recv, b2_s, b2_r)

    wait_bytes(kb_recv.at[0, pl.ds(0, 3)], kb_r)
    forward = remote(kb_recv.at[core], kb_recv.at[core], kf_s, kf_r, (s + 1 - 2 * core, e))
    forward.start()
    forward.wait()
    for src in range(SEQ):
        got = kb_recv[src % 2, src // 2]
        kfull[ROWS * src : ROWS * src + PACK, WINDOW:128] = got[:PACK, :WINDOW]
        kfull[ROWS * src + PACK : ROWS * (src + 1), WINDOW:128] = got[:PACK, WINDOW:]
        kfull[ROWS * src : ROWS * (src + 1), 128:] = got[PACK:]
    every = jnp.dot(tok[...], kfull[...], preferred_element_type=F32)
    up = jnp.exp(every - jnp.max(every, axis=1, keepdims=True))
    natural = (up[:, :WINDOW] * (1.0 / jnp.sum(up, axis=1, keepdims=True))).astype(BF)
    k = lax.broadcasted_iota(jnp.int32, (WINDOW, WINDOW), 0)
    g = lax.broadcasted_iota(jnp.int32, (WINDOW, WINDOW), 1)
    hit = g == lax.rem(k // SIDE + lax.rem(k, SIDE), SIDE) * SIDE + lax.rem(k, SIDE)
    comb[...] = jnp.dot(natural, jnp.where(hit, 1.0, 0.0).astype(BF), preferred_element_type=F32).astype(BF)

    wait_bytes(ka_recv.at[pl.ds(0, SEQ - 1)], ka_s)
    wait_bytes(kb_recv.at[0, pl.ds(0, 3)], kb_s)
    wait_bytes(st_recv.at[pl.ds(0, SEQ - 1)], st_s)
    wait_bytes(p_recv.at[pl.ds(0, SEQ - 1)], p_s)
    wait_bytes(q_recv.at[pl.ds(0, SEQ - 1)], q_s)
    exchanged(c1_recv, b1_s)
    wait_bytes(c1_recv.at[0], c1_s)
    share(c2_recv, b2_r, c2_s, c2_r)
    gather_lines(mixed_in)
    exchanged(c2_recv, b2_s)
    wait_bytes(c2_recv.at[0], c2_s)


def mix_kernel(comb, rows, out_hbm, outv, sem):
    copies = []
    for c in range(5):
        cols = slice(256 * c, 256 * (c + 1))
        outv[:, cols] = jnp.dot(comb[...], rows[:, cols], preferred_element_type=F32).astype(BF)
        copies.append(pltpu.make_async_copy(outv.at[:, cols], out_hbm.at[0, :, cols], sem.at[c]))
        copies[-1].start()
    for copy in copies:
        copy.wait()


def on_device(tokens, slot_keys, expert_in, expert_out):
    dma = pltpu.SemaphoreType.DMA
    reg = pltpu.SemaphoreType.REGULAR
    vm = pltpu.VMEM
    lines, folded = (SIDE * LINE, 128), (SEQ, 16, HALF)
    scratch = [
        vm((PATCH, D), BF), vm((ROWS, SLOTS), BF), vm((D, HID), BF), vm((HID, D), BF),
        vm((PACK, 128), BF), vm((SEQ, PACK, 128), BF), vm((REST, 128), BF), vm((2, 4, REST, 128), BF), vm((D, SLOTS), BF),
        vm((WINDOW, 128), F32), vm((SEQ, SIDE, 128), F32), vm(folded, BF), vm(folded, BF), vm(folded, BF), vm(folded, BF),
        vm(((SIDE + 1) * LINE, 128), F32), vm((65 * LINE, 128), F32), vm(lines, BF), vm(lines, BF),
        vm((2, 32 * LINE, 128), BF), vm((2, 32 * LINE, 128), BF), vm((64, D), BF),
        dma((4,)), reg, reg, reg, reg,
    ] + [dma] * 20
    operands = [pltpu.with_memory_space_constraint(a, pltpu.HBM) for a in (tokens, slot_keys, expert_in, expert_out)]
    in_vmem = pl.BlockSpec(memory_space=pltpu.VMEM)
    anywhere = pl.BlockSpec(memory_space=pl.ANY)
    comb, rows = pl.pallas_call(
        kernel,
        name="moe",
        out_shape=(jax.ShapeDtypeStruct((PATCH, WINDOW), BF), jax.ShapeDtypeStruct((64, D), BF)),
        in_specs=[anywhere] * 4,
        out_specs=(in_vmem, in_vmem),
        scratch_shapes=scratch,
        compiler_params=pltpu.CompilerParams(collective_id=0, has_side_effects=True, vmem_limit_bytes=48 * 1024 * 1024),
    )(*operands)
    return pl.pallas_call(
        mix_kernel,
        name="mix",
        out_shape=jax.ShapeDtypeStruct(tokens.shape, BF),
        in_specs=[in_vmem, in_vmem],
        out_specs=anywhere,
        scratch_shapes=[vm((PATCH, D), BF), dma((5,))],
        compiler_params=pltpu.CompilerParams(vmem_limit_bytes=48 * 1024 * 1024),
    )(comb, rows)


def solution(mesh):
    return jax.shard_map(
        on_device,
        mesh=mesh,
        in_specs=(
            P("exp", "seq", None),
            P("seq", None),
            P("exp", None, "seq"),
            P("exp", "seq", None),
        ),
        out_specs=P("exp", "seq", None),
        check_vma=False,
    )
```

```python
import jax
import jax.numpy as jnp
from jax import lax
from jax.experimental import pallas as pl
from jax.experimental.pallas import tpu as pltpu
from jax.sharding import PartitionSpec as P

MESH = pl.DeviceIdType.MESH
BF = jnp.bfloat16
F32 = jnp.float32
SEQ = 8
SIDE = 8
D = 1280
HID = 640
PATCH = 256
SLOTS = 256
WINDOW = 64
ROWS = D // SEQ
HALF = D // 2
PACK = ROWS // 2
REST = PACK + ROWS
LINE = 16
TILES = D // 128
NEAR = (4, 5, 3, 6, 2, 7, 1)


def wait_bytes(ref, sem):
    pltpu.make_async_copy(ref, ref, sem).wait()


def gelu(v):
    inner = 0.7978845608028654 * (v + 0.044715 * (v * v * v))
    return 0.5 * v * (1.0 + jnp.tanh(inner))


def kernel(
    tok_hbm, keys_hbm, w1_hbm, w2_hbm, comb, mixed_in,
    tok, keys, w1, w2,
    ka_send, ka_recv, kb_send, kb_recv, kfull,
    st_send, st_recv, p_send, p_recv, q_send, q_recv,
    stage, wide, r1_send, r2_send, c1_recv, c2_recv, xv,
    load_sem, ysem, rsem, zsem, wsem,
    ka_s, ka_r, kb_s, kb_r, kf_s, kf_r, st_s, st_r, p_s, p_r, q_s, q_r,
    b1_s, b1_r, b2_s, b2_r, c1_s, c1_r, c2_s, c2_r,
):
    s = lax.axis_index("seq")
    e = lax.axis_index("exp")
    x, core = s // 2, lax.rem(s, 2)
    z, y = e // SIDE, lax.rem(e, SIDE)
    skew = lax.rem(z + y, SIDE)
    mine = lax.rem(s - skew + SIDE, SIDE)

    def along_y(d):
        return (s, z * SIDE + lax.rem(y + d, SIDE))

    def along_z(d):
        return (s, lax.rem(z + d, SIDE) * SIDE + y)

    def along_seq(d):
        return (lax.rem(s + d, SEQ), e)

    def signal(sem, device):
        pl.semaphore_signal(sem, inc=1, device_id=device, device_id_type=MESH)

    def remote(src, dst, ssem, rsem, device):
        return pltpu.make_async_remote_copy(
            src_ref=src, dst_ref=dst, send_sem=ssem, recv_sem=rsem, device_id=device, device_id_type=MESH
        )

    def group_of(d):
        return lax.rem(s + d - skew + SIDE, SIDE)

    loads = [
        pltpu.make_async_copy(keys_hbm, keys, load_sem.at[0]),
        pltpu.make_async_copy(tok_hbm.at[0], tok, load_sem.at[1]),
        pltpu.make_async_copy(w1_hbm.at[0], w1, load_sem.at[2]),
        pltpu.make_async_copy(w2_hbm.at[0], w2, load_sem.at[3]),
    ]
    loads[0].start()
    barrier = pltpu.get_barrier_semaphore()
    for d in NEAR:
        signal(barrier, along_seq(d))
    for d in (2, 6, 1, 7):
        signal(barrier, along_y(d))
        signal(barrier, along_z(d))
    for load in loads[1:]:
        load.start()
    stage[...] = jnp.zeros_like(stage)

    loads[0].wait()
    kk = keys[...]
    ka = jnp.concatenate([kk[:PACK, :WINDOW], kk[PACK:, :WINDOW]], axis=1)
    ka_send[...] = ka
    ka_recv[s] = ka
    kb_send[:PACK] = jnp.concatenate([kk[:PACK, WINDOW:128], kk[PACK:, WINDOW:128]], axis=1)
    kb_send[PACK:] = kk[:, 128:]
    kb_recv[core, x] = kb_send[...]
    pl.semaphore_wait(barrier, 15)
    for d in NEAR:
        remote(ka_send, ka_recv.at[s], ka_s, ka_r, along_seq(d)).start()
    for d in (2, 6, 1, 7):
        signal(ysem, along_y(d))
    for d in (2, 6):
        signal(zsem, along_z(d))
    pl.semaphore_wait(ysem, 4)
    for d in (2, 6):
        signal(rsem, along_y(d))
    loads[1].wait()
    wait_bytes(ka_recv.at[pl.ds(0, SEQ - 1)], ka_r)
    for src in range(SEQ):
        got = ka_recv[src]
        kfull[ROWS * src : ROWS * src + PACK, :WINDOW] = got[:, :WINDOW]
        kfull[ROWS * src + PACK : ROWS * (src + 1), :WINDOW] = got[:, WINDOW:]

    scores = jnp.dot(tok[...], kfull[:, :WINDOW], preferred_element_type=F32)
    scores_t = scores.T
    place = lax.rem(lax.broadcasted_iota(jnp.int32, (SIDE, PATCH), 0), SIDE)
    groups = []
    for g in range(SIDE):
        block = scores_t[g * SIDE : (g + 1) * SIDE]
        for yk in range(1, SIDE):
            zk = (g - yk) % SIDE
            block = jnp.where(place == yk, scores_t[zk * SIDE : (zk + 1) * SIDE], block)
        groups.append(block)
    scores_t = jnp.concatenate(groups, axis=0)
    top = jnp.max(scores_t, axis=1, keepdims=True)
    raised = jnp.exp(scores_t - top)
    total = jnp.sum(raised, axis=1, keepdims=True)
    lane = lax.broadcasted_iota(jnp.int32, (WINDOW, 128), 1)
    st_send[...] = jnp.where(lane < 64, top, total)
    for d in NEAR:
        rows = pl.ds(pl.multiple_of(group_of(d) * SIDE, SIDE), SIDE)
        remote(st_send.at[rows], st_recv.at[s], st_s, st_r, along_seq(d)).start()
    st_recv[s] = st_send[pl.ds(pl.multiple_of(mine * SIDE, SIDE), SIDE)]
    pl.semaphore_wait(rsem, 2)
    pl.semaphore_wait(zsem, 2)
    for d in NEAR:
        signal(wsem, along_z(d))

    part = jnp.dot(raised.astype(BF), tok[...], preferred_element_type=F32)
    part = part * (1.0 / total)

    def fold(values, ref):
        for g in range(SIDE):
            block = values[g * SIDE : (g + 1) * SIDE]
            ref[g] = jnp.concatenate([block[:, :HALF], block[:, HALF:]], axis=0).astype(BF)

    def to_owners(send, recv, ssem, rsem):
        for d in NEAR:
            remote(send.at[group_of(d)], recv.at[s], ssem, rsem, along_seq(d)).start()
        recv[s] = send[mine]

    def line(row):
        return pl.ds(pl.multiple_of(row * LINE, LINE), LINE)

    def exchange(low, high, send, recv, ssem, rsem):
        for t in range(TILES):
            half = low if t < TILES // 2 else high
            c = (t % (TILES // 2)) * 128
            stage[pl.ds(t, SIDE, stride=LINE), :] = half[:, c : c + 128]
        send[...] = stage[: SIDE * LINE].astype(BF)
        here = recv.at[lax.rem(skew, 2), line((skew // 2) * SIDE + y)]
        for d in NEAR + (0,):
            row = lax.rem(y + d, SIDE)
            place = lax.rem(mine - row + SIDE, SIDE) * SIDE + row
            for dx in (2, 1, 3, 0):
                if d or dx:
                    to = (lax.rem(x + dx, 4) * 2 + core, place)
                    remote(send.at[line(row)], here, ssem, rsem.at[skew // 2], to).start()

        @pl.when(mine != skew)
        def _():
            remote(send.at[line(y)], here, ssem, rsem.at[skew // 2], (s, lax.rem(mine - y + SIDE, SIDE) * SIDE + y)).start()

        @pl.when(mine == skew)
        def _():
            pltpu.make_async_copy(send.at[line(y)], here, rsem.at[skew // 2]).start()

    def exchanged(recv, ssem):
        @pl.when(mine != skew)
        def _():
            wait_bytes(recv.at[0], ssem)

        @pl.when(mine == skew)
        def _():
            wait_bytes(recv.at[0, pl.ds(0, 31 * LINE)], ssem)

    def share(recv, rsem, ssem, csem):
        own = lax.rem(core + skew, 2)
        for dx in (0, 1, 3, 2):
            g = lax.rem(2 * lax.rem(x + dx, 4) + core - own - skew + 16, SIDE) // 2
            eight = recv.at[own, pl.ds(pl.multiple_of(g * SIDE * LINE, SIDE * LINE), SIDE * LINE)]
            wait_bytes(eight, rsem.at[g])
            remote(eight, eight, ssem, csem, (s + 1 - 2 * core, e)).start()
        wide[pl.ds(pl.multiple_of(own * 32 * LINE, 32 * LINE), 32 * LINE)] = recv[own].astype(F32)
        other = 1 - own
        wait_bytes(recv.at[other], csem)
        wide[pl.ds(pl.multiple_of(other * 32 * LINE, 32 * LINE), 32 * LINE)] = recv[other].astype(F32)

    def gather_lines(ref):
        for t in range(TILES):
            tile = wide[pl.ds(t, 64, stride=LINE), :]
            groups = [tile[SIDE * ((g % 2) * 4 + g // 2) :][:SIDE] for g in range(SIDE)]
            ref[:, 128 * t : 128 * (t + 1)] = jnp.concatenate(groups, axis=0).astype(BF)

    fold(part, p_send)
    to_owners(p_send, p_recv, p_s, p_r)

    wait_bytes(st_recv.at[pl.ds(0, SEQ - 1)], st_r)
    tops = [st_recv[i][:, 0:1] for i in range(SEQ)]
    sums = [st_recv[i][:, 64:65] for i in range(SEQ)]
    peak = tops[0]
    for i in range(1, SEQ):
        peak = jnp.maximum(peak, tops[i])
    weights = [jnp.exp(tops[i] - peak) * sums[i] for i in range(SEQ)]
    norm = weights[0]
    for i in range(1, SEQ):
        norm = norm + weights[i]
    norm = 1.0 / norm

    pl.semaphore_wait(wsem, 7)
    wait_bytes(p_recv.at[pl.ds(0, SEQ - 1)], p_r)
    low = high = None
    for i in range(SEQ):
        got = p_recv[i].astype(F32)
        w = weights[i] * norm
        a, b = got[:SIDE] * w, got[SIDE:] * w
        low, high = (a, b) if low is None else (low + a, high + b)
    exchange(low, high, r1_send, c1_recv, b1_s, b1_r)
    for d in (4, 2, 6):
        remote(kb_send, kb_recv.at[core, x], kb_s, kb_r, along_seq(d)).start()
    loads[2].wait()
    loads[3].wait()
    share(c1_recv, b1_r, c1_s, c1_r)

    gather_lines(xv)
    hidden = gelu(jnp.dot(xv[...], w1[...], preferred_element_type=F32)).astype(BF)
    fold(jnp.dot(hidden, w2[...], preferred_element_type=F32), q_send)
    to_owners(q_send, q_recv, q_s, q_r)
    wait_bytes(q_recv.at[pl.ds(0, SEQ - 1)], q_r)
    low = high = None
    for i in range(SEQ):
        got = q_recv[i].astype(F32)
        a, b = got[:SIDE], got[SIDE:]
        low, high = (a, b) if low is None else (low + a, high + b)
    exchange(low, high, r2_send, c2_recv, b2_s, b2_r)

    wait_bytes(kb_recv.at[0, pl.ds(0, 3)], kb_r)
    forward = remote(kb_recv.at[core], kb_recv.at[core], kf_s, kf_r, (s + 1 - 2 * core, e))
    forward.start()
    forward.wait()
    for src in range(SEQ):
        got = kb_recv[src % 2, src // 2]
        kfull[ROWS * src : ROWS * src + PACK, WINDOW:128] = got[:PACK, :WINDOW]
        kfull[ROWS * src + PACK : ROWS * (src + 1), WINDOW:128] = got[:PACK, WINDOW:]
        kfull[ROWS * src : ROWS * (src + 1), 128:] = got[PACK:]
    every = jnp.dot(tok[...], kfull[...], preferred_element_type=F32)
    up = jnp.exp(every - jnp.max(every, axis=1, keepdims=True))
    natural = (up[:, :WINDOW] * (1.0 / jnp.sum(up, axis=1, keepdims=True))).astype(BF)
    k = lax.broadcasted_iota(jnp.int32, (WINDOW, WINDOW), 0)
    g = lax.broadcasted_iota(jnp.int32, (WINDOW, WINDOW), 1)
    hit = g == lax.rem(k // SIDE + lax.rem(k, SIDE), SIDE) * SIDE + lax.rem(k, SIDE)
    comb[...] = jnp.dot(natural, jnp.where(hit, 1.0, 0.0).astype(BF), preferred_element_type=F32).astype(BF)

    wait_bytes(ka_recv.at[pl.ds(0, SEQ - 1)], ka_s)
    wait_bytes(kb_recv.at[0, pl.ds(0, 3)], kb_s)
    wait_bytes(st_recv.at[pl.ds(0, SEQ - 1)], st_s)
    wait_bytes(p_recv.at[pl.ds(0, SEQ - 1)], p_s)
    wait_bytes(q_recv.at[pl.ds(0, SEQ - 1)], q_s)
    exchanged(c1_recv, b1_s)
    wait_bytes(c1_recv.at[0], c1_s)
    share(c2_recv, b2_r, c2_s, c2_r)
    gather_lines(mixed_in)
    exchanged(c2_recv, b2_s)
    wait_bytes(c2_recv.at[0], c2_s)


def mix_kernel(comb, rows, out_hbm, outv, sem):
    copies = []
    for c in range(5):
        cols = slice(256 * c, 256 * (c + 1))
        outv[:, cols] = jnp.dot(comb[...], rows[:, cols], preferred_element_type=F32).astype(BF)
        copies.append(pltpu.make_async_copy(outv.at[:, cols], out_hbm.at[0, :, cols], sem.at[c]))
        copies[-1].start()
    for copy in copies:
        copy.wait()


def on_device(tokens, slot_keys, expert_in, expert_out):
    dma = pltpu.SemaphoreType.DMA
    reg = pltpu.SemaphoreType.REGULAR
    vm = pltpu.VMEM
    lines, folded = (SIDE * LINE, 128), (SEQ, 16, HALF)
    scratch = [
        vm((PATCH, D), BF), vm((ROWS, SLOTS), BF), vm((D, HID), BF), vm((HID, D), BF),
        vm((PACK, 128), BF), vm((SEQ, PACK, 128), BF), vm((REST, 128), BF), vm((2, 4, REST, 128), BF), vm((D, SLOTS), BF),
        vm((WINDOW, 128), F32), vm((SEQ, SIDE, 128), F32), vm(folded, BF), vm(folded, BF), vm(folded, BF), vm(folded, BF),
        vm(((SIDE + 1) * LINE, 128), F32), vm((65 * LINE, 128), F32), vm(lines, BF), vm(lines, BF),
        vm((2, 32 * LINE, 128), BF), vm((2, 32 * LINE, 128), BF), vm((64, D), BF),
        dma((4,)), reg, reg, reg, reg,
    ] + [dma] * 13 + [dma((4,)), dma, dma((4,))] + [dma] * 4
    operands = [pltpu.with_memory_space_constraint(a, pltpu.HBM) for a in (tokens, slot_keys, expert_in, expert_out)]
    in_vmem = pl.BlockSpec(memory_space=pltpu.VMEM)
    anywhere = pl.BlockSpec(memory_space=pl.ANY)
    comb, rows = pl.pallas_call(
        kernel,
        name="moe",
        out_shape=(jax.ShapeDtypeStruct((PATCH, WINDOW), BF), jax.ShapeDtypeStruct((64, D), BF)),
        in_specs=[anywhere] * 4,
        out_specs=(in_vmem, in_vmem),
        scratch_shapes=scratch,
        compiler_params=pltpu.CompilerParams(collective_id=0, has_side_effects=True, vmem_limit_bytes=48 * 1024 * 1024),
    )(*operands)
    return pl.pallas_call(
        mix_kernel,
        name="mix",
        out_shape=jax.ShapeDtypeStruct(tokens.shape, BF),
        in_specs=[in_vmem, in_vmem],
        out_specs=anywhere,
        scratch_shapes=[vm((PATCH, D), BF), dma((5,))],
        compiler_params=pltpu.CompilerParams(vmem_limit_bytes=48 * 1024 * 1024),
    )(comb, rows)


def solution(mesh):
    return jax.shard_map(
        on_device,
        mesh=mesh,
        in_specs=(
            P("exp", "seq", None),
            P("seq", None),
            P("exp", None, "seq"),
            P("exp", "seq", None),
        ),
        out_specs=P("exp", "seq", None),
        check_vma=False,
    )
```
